256 devices in a mesh: slab: 64 (over x, z, core), col: 4 (over y).
Axes of the slice: x: 4, y: 4, z: 8, core: 2. Of those that a mesh axis runs over, the one named last changes fastest.
Arguments:
- pressure: float32 [4096, 1024], P('slab', 'col'), may hold values from 1 to 4
- storage: float32 [4096, 1024], P('slab', 'col'), may hold values from 0.5 to 2
- trans: float32 [4096, 1024], P('slab', 'col'), may hold values from 0.5 to 8
- source: float32 [4096, 1024], P('slab', 'col'), may hold values from -1.2 to 1.2
- shells_old: float32 [4, 4096, 64, 128], P('col', 'slab'), may hold values from 1 to 2
- shell_cap: float32 [64], replicated, may hold values from 0.5 to 4
- shell_trans: float32 [64], replicated, may hold values from 0.5 to 4
- new_source: int32 [4, 2048], P('col'), may hold values from 0 to 4095, as said below
- cell_block: int32 [4, 4096], P('col', 'slab'), may hold values from 0 to 127, as said below
Outputs:
- pressure_out: float32 [4096, 1024], P('slab', 'col')
- shells_new: float32 [4, 2048, 64, 128], P('col', 'slab')
The draws below stay inside these ranges and needn't reach their ends.
Inputs may be any that keep to these rules, and one draw needn't show every extreme that they name: `new_source`: within each col index, every old slot is taken at most once; the slots after the move on one slab device take blocks from 8 distinct slab devices, exactly 4 blocks from each; the taken old slots lie only on the even-numbered slab devices, each of which has all 64 of its slots taken. `cell_block`: within one slab device and col index the entries are distinct.
All inputs are finite; a program needn't handle non-finite values.
Results may differ from the reference program's by a relative error of at most 0.0003.
Values sent between devices are 32-bit elements; how exact they have to be, the bound alone decides.
A program may use at most 128 MiB of HBM per device.

```python
import math
import jax
import jax.numpy as jnp
from jax import lax

CS = 64
CW = 256
CB = 128
SH = 64
CAP = 4
B_NEW = 32
STEPS = 2
ITERS = 3
B_OLD = 64
FB = 128
NX = 4096
NY = 1024
NOLD = 4096
N_SLAB = 64
N_COL = 4


def draw_new_source(key, part):

    def one_col(col_key):
        key_order, key_old, key_new = jax.random.split(col_key, 3)
        order = jax.random.permutation(key_order, N_SLAB)
        shuffle_old = jax.random.permutation(key_old, B_OLD)
        shuffle_new = jax.random.permutation(key_new, B_NEW)
        half = N_SLAB // 2
        groups = B_NEW // CAP
        position = jnp.arange(N_SLAB)
        group_index = jnp.arange(groups)
        within = jnp.arange(CAP)
        source_dev = 2 * ((position[:, None] // 2 + group_index[None, :]) % half)
        group_old = 2 * group_index[None, :] + position[:, None] % 2
        local = shuffle_old[group_old[:, :, None] * CAP + within[None, None, :]]
        global_slot = source_dev[:, :, None] * B_OLD + local
        by_position = global_slot.reshape(N_SLAB, B_NEW)[:, shuffle_new]
        placed = jnp.zeros((N_SLAB, B_NEW), jnp.int32).at[order].set(by_position.astype(jnp.int32))
        return placed.reshape(-1)
    keys = jax.random.split(jax.random.fold_in(key, 11), N_COL)
    return jax.vmap(one_col)(keys).astype(jnp.int32)


def draw_cell_block(key, part):
    keys = jax.random.split(jax.random.fold_in(key, 23), N_COL * N_SLAB)
    chosen = jax.vmap(lambda one_key: jax.random.permutation(one_key, FB)[:B_OLD])(keys)
    return chosen.reshape(N_COL, N_SLAB * B_OLD).astype(jnp.int32)


def level_of(own_key, dims, pieces, low, largest):
    level, own = 1.0, jax.random.fold_in(own_key, 6)
    for dim, blocks in pieces:
        steps = jnp.exp(jax.random.uniform(jax.random.fold_in(own, dim), (blocks,), jnp.float32, low / len(pieces), largest / len(pieces)))
        level = level * jnp.repeat(steps, dims[dim] // blocks).reshape([-1 if axis == dim else 1 for axis in range(len(dims))])
    return level


def normal_values(own_key, extent, spread, bound, pieces=(), held_as=jnp.bfloat16):
    result = jax.random.normal(own_key, extent, jnp.float32) * spread
    if len(pieces) > 0:
        result = level_of(own_key, extent, pieces, -0.22, 0.18) * result
    return jnp.clip(result, min=-bound, max=bound).astype(held_as)


def setup_inputs(seed: int = 0) -> dict:
    splits = jax.random.split(jax.random.key(seed), 10)
    pressure = jnp.clip(1.0 + 3.0 * jax.random.uniform(splits[0], (NX, NY), jnp.float32) ** level_of(splits[0], (NX, NY), ((0, 64), (1, 4)), -0.2, 0.2), 1.0, 4.0)
    storage = jnp.clip(jnp.exp(math.log(2.0) - 1.3862944 * jax.random.uniform(splits[1], (NX, NY), jnp.float32) ** level_of(splits[1], (NX, NY), ((0, 64), (1, 4)), -0.2, 0.2)), 0.5, 2.0)
    trans = jnp.clip(jnp.exp(math.log(8.0) - 2.7725887 * jax.random.uniform(splits[2], (NX, NY), jnp.float32) ** level_of(splits[2], (NX, NY), ((0, 64), (1, 4)), -0.2, 0.2)), 0.5, 8.0)
    source = normal_values(splits[3], (NX, NY), 0.25, 1.2, ((0, 64), (1, 4)), jnp.float32)
    shells_old = jnp.clip(1.0 + 1.0 * jax.random.uniform(splits[4], (N_COL, NOLD, SH, CB), jnp.float32) ** level_of(splits[4], (N_COL, NOLD, SH, CB), ((0, 4), (1, 64)), -0.2, 0.2), 1.0, 2.0)
    shell_cap = jnp.clip(jnp.exp(jax.random.uniform(splits[5], (SH,), jnp.float32, math.log(0.5), math.log(4.0))), 0.5, 4.0)
    shell_trans = jnp.clip(jnp.exp(jax.random.uniform(splits[6], (SH,), jnp.float32, math.log(0.5), math.log(4.0))), 0.5, 4.0)
    new_source = draw_new_source(jax.random.fold_in(splits[9], 71), 0)
    cell_block = draw_cell_block(jax.random.fold_in(splits[9], 71), 0)
    return dict(pressure=pressure, storage=storage, trans=trans, source=source, shells_old=shells_old, shell_cap=shell_cap, shell_trans=shell_trans, new_source=new_source, cell_block=cell_block)


def shell_inverse(shell_cap, shell_trans):
    inner = jnp.concatenate([shell_trans[1:], jnp.zeros((1,), jnp.float32)])
    matrix = jnp.diag(shell_cap + shell_trans + inner) - jnp.diag(inner[:-1], 1) - jnp.diag(inner[:-1], -1)
    inverse = jnp.linalg.solve(matrix, jnp.eye(matrix.shape[0], dtype=jnp.float32))
    return (inverse, inverse[:, 0] * shell_trans[0])

def newton_update(pressure, padded, tpad, prev, storage, source, exchange_term, active, coupling):
    height, breadth = pressure.shape
    center = tpad[1:-1, 1:-1]
    flux = jnp.zeros_like(pressure)
    conduct = jnp.zeros_like(pressure)
    for shift_row, shift_col in ((0, 1), (2, 1), (1, 0), (1, 2)):
        near_p = padded[shift_row:shift_row + height, shift_col:shift_col + breadth]
        near_t = tpad[shift_row:shift_row + height, shift_col:shift_col + breadth]
        face = 2.0 * center * near_t / (center + near_t)
        flux = flux + face * 0.5 * (near_p + pressure) * (near_p - pressure)
        conduct = conduct + face
    misfit = storage * (pressure - prev) - flux + exchange_term - source
    slope = storage + pressure * conduct + active * coupling
    return pressure - misfit / slope

def reference(pressure, storage, trans, source, shells_old, shell_cap, shell_trans, new_source, cell_block):
    inverse, couple = shell_inverse(shell_cap, shell_trans)
    coupling = shell_trans[0] * (1.0 - couple[0])
    ncols = new_source.shape[0]
    per_row = CW // 128
    home = new_source // B_OLD
    fblock = jax.vmap(lambda table, index: table[index])(cell_block, new_source)
    row_of = home * CS + fblock // per_row
    start = jnp.arange(ncols, dtype=jnp.int32)[:, None] * CW + fblock % per_row * 128
    flat = ((row_of * NY + start)[..., None] + jnp.arange(CB, dtype=jnp.int32)).astype(jnp.int32)
    flat_all = flat.reshape(-1)
    state = jax.vmap(lambda table, index: table[index])(shells_old, new_source)
    active = jnp.zeros((NX * NY,), jnp.float32).at[flat_all].set(1.0).reshape(NX, NY)
    tpad = jnp.pad(trans, 1)
    current = pressure
    for step in range(STEPS):
        prev = current
        for sweep in range(ITERS):
            block_p = current.reshape(-1)[flat]
            scaled = shell_cap[None, None, :, None] * state
            shells = jnp.einsum('kl,nblc->nbkc', inverse, scaled, precision=lax.Precision.HIGHEST)
            shells = shells + couple[None, None, :, None] * block_p[:, :, None, :]
            flow = shell_trans[0] * (block_p - shells[:, :, 0, :])
            exchange_term = jnp.zeros((NX * NY,), jnp.float32).at[flat_all].add(flow.reshape(-1)).reshape(NX, NY)
            current = newton_update(current, jnp.pad(current, 1), tpad, prev, storage, source, exchange_term, active, coupling)
        state = shells
    return (current, state)
```

```python
import jax
import jax.numpy as jnp
from jax import lax
from jax.sharding import PartitionSpec as P

CAP = 4
STEPS = 2
ITERS = 3
HI = lax.Precision.HIGHEST


def with_halo(shard, sides, width):
    for axis, dim in sides:
        size, length = (lax.axis_size(axis), shard.shape[dim])
        up = [(i, (i + 1) % size) for i in range(size - 1)]
        down = [(j, i) for i, j in up]
        last = lax.slice_in_dim(shard, length - width, length, axis=dim)
        initial = lax.slice_in_dim(shard, 0, width, axis=dim)
        before = lax.ppermute(last, axis, up)
        after = lax.ppermute(initial, axis, down)
        shard = jnp.concatenate([before, shard, after], axis=dim)
    return shard


def shift_rows(x, s):
    z = jnp.zeros((abs(s),) + x.shape[1:], x.dtype)
    return jnp.concatenate([z, x[:-s]], 0) if s > 0 else jnp.concatenate([x[-s:], z], 0)


def shell_inverse(cap, tr):
    n = cap.shape[0]
    inner = jnp.concatenate([tr[1:], jnp.zeros((1,), jnp.float32)])
    b = (cap + tr + inner)[:, None]
    c = -inner[:, None]
    a = jnp.concatenate([jnp.zeros((1, 1), jnp.float32), c[:-1]], 0)
    rhs = jnp.eye(n, dtype=jnp.float32)
    one = jnp.ones_like(b)
    s = 1
    while s < n:
        bm = jnp.concatenate([one[:s], b[:-s]], 0)
        bp = jnp.concatenate([b[s:], one[:s]], 0)
        al, ga = -a / bm, -c / bp
        rhs = rhs + al * shift_rows(rhs, s) + ga * shift_rows(rhs, -s)
        b = b + al * shift_rows(c, s) + ga * shift_rows(a, -s)
        a, c = al * shift_rows(a, s), ga * shift_rows(c, -s)
        s *= 2
    inverse = rhs / b
    return inverse, inverse[:, 0] * tr[0]


def shards(pressure, storage, trans, source, shells_old, shell_cap, shell_trans, new_source, cell_block):
    slab_count = lax.axis_size("slab")
    own = lax.axis_index("slab")
    height, breadth = pressure.shape
    old_slots = shells_old.shape[1]
    nsh = shells_old.shape[2]
    table = new_source[0]
    new_slots = table.shape[0] // slab_count
    inverse, couple = shell_inverse(shell_cap, shell_trans)
    coupling = shell_trans[0] * (1.0 - couple[0])
    amat = inverse * shell_cap[None, :]
    asq = jnp.dot(amat, amat, precision=HI)
    acouple = jnp.dot(amat, couple, precision=HI)
    anchor = (table // old_slots).reshape(slab_count, new_slots)
    local_old = (table % old_slots).reshape(slab_count, new_slots)
    hit = anchor == own
    earlier = jnp.arange(new_slots)[:, None] < jnp.arange(new_slots)[None, :]
    before = jnp.sum(hit[:, :, None] & earlier[None], 1)
    slot = jnp.stack([jnp.sum(jnp.where(hit & (before == r), local_old, 0), 1) for r in range(CAP)], 1)
    own_anchor = lax.dynamic_index_in_dim(anchor, own, 0, keepdims=False)
    idx = jnp.arange(new_slots)
    own_rank = jnp.sum((own_anchor[:, None] == own_anchor[None, :]) & (idx[:, None] > idx[None, :]), 1)
    recv_pos = own_anchor * CAP + own_rank
    state = shells_old[0]
    even = (own % 2 == 0).astype(jnp.float32)
    cb = cell_block[0]
    onehot = (cb[None, :] == jnp.arange(height * breadth // 128)[:, None]).astype(jnp.float32) * even
    rows = jnp.einsum("rk,okc->roc", jnp.stack([amat[0], asq[0]]), state, precision=HI) * shell_trans[0]
    spread = jnp.einsum("fo,roc->rfc", onehot, rows, precision=HI).reshape(2, height, breadth)
    ak = jnp.broadcast_to(jnp.sum(onehot, 1)[:, None] * coupling, (onehot.shape[0], 128)).reshape(height, breadth)
    c2 = shell_trans[0] * jnp.dot(amat[0], couple, precision=HI)
    act = jnp.broadcast_to(jnp.sum(onehot, 1)[:, None], (onehot.shape[0], 128)).reshape(height, breadth)
    tpad = with_halo(trans, (("slab", 0), ("col", 1)), 1)
    shifts = ((0, 1), (2, 1), (1, 0), (1, 2))
    faces = []
    for r, c in shifts:
        near = tpad[r : r + height, c : c + breadth]
        faces.append(2.0 * trans * near / (trans + near))
    conduct = faces[0] + faces[1] + faces[2] + faces[3]
    current = pressure
    saved = []
    for step in range(STEPS):
        prev = current
        base = spread[0] if step == 0 else spread[1] + act * c2 * saved[0]
        for sweep in range(ITERS):
            if sweep == ITERS - 1:
                saved.append(current)
            padded = with_halo(current, (("slab", 0), ("col", 1)), 1)
            flux = jnp.zeros_like(current)
            for (r, c), face in zip(shifts, faces):
                near = padded[r : r + height, c : c + breadth]
                flux = flux + face * 0.5 * (near + current) * (near - current)
            misfit = storage * (current - prev) - flux + (ak * current - base) - source
            current = current - misfit / (storage + current * conduct + ak)
    pb = [jnp.dot(onehot.T, s.reshape(-1, 128), precision=HI) for s in saved]
    final = jnp.einsum("kl,olc->okc", asq, state, precision=HI)
    final = final + acouple[None, :, None] * pb[0][:, None] + couple[None, :, None] * pb[1][:, None]
    pick = (slot.reshape(-1, 1) == jnp.arange(old_slots)[None, :]).astype(jnp.float32)
    outgoing = jnp.dot(pick, final.reshape(old_slots, -1), precision=HI).reshape(slab_count, CAP, nsh, 128)
    arrived = lax.all_to_all(outgoing, "slab", split_axis=0, concat_axis=0, tiled=True)
    take = (recv_pos[:, None] == jnp.arange(slab_count * CAP)[None, :]).astype(jnp.float32)
    out = jnp.dot(take, arrived.reshape(slab_count * CAP, -1), precision=HI).reshape(new_slots, nsh, 128)
    return current, out[None]


def solution(mesh):
    f = P("slab", "col")
    return jax.shard_map(
        shards,
        mesh=mesh,
        in_specs=(f, f, f, f, P("col", "slab", None, None), P(), P(), P("col", None), P("col", "slab")),
        out_specs=(f, P("col", "slab", None, None)),
        check_vma=False,
    )
```

```python
import functools

import jax
import jax.numpy as jnp
from jax import lax
from jax.experimental import pallas as pl
from jax.experimental.pallas import tpu as pltpu
from jax.sharding import PartitionSpec as P

MESH = pl.DeviceIdType.MESH
HI = lax.Precision.HIGHEST
F32, I32 = jnp.float32, jnp.int32
SLABS = 64
CHIPS = 32
SH = 64
NEW = 32
OLD = 64
STEPS, ITERS = 2, 3
IDX2, IDX3 = 16, 24


def iota(shape, dim):
    return lax.broadcasted_iota(I32, shape, dim)


def strict_upper(n):
    return (iota((n, n), 0) < iota((n, n), 1)).astype(F32)


def route(own, tab, out_ref):
    chip, local = tab >> 7, tab & 63
    n_of, lane32 = iota((NEW, 128), 0), iota((NEW, 128), 1)
    rank = jnp.zeros((NEW, 128), I32)
    for k in range(1, NEW):
        rank = rank + ((pltpu.roll(chip, k, 0) == chip) & (n_of >= k)).astype(I32)
    s_of = n_of
    feeds = jnp.zeros((CHIPS, 128), jnp.bool_)
    for n in range(NEW):
        feeds = feeds | (s_of == chip[n : n + 1, :])
    feeds_f = feeds.astype(F32)
    upper = strict_upper(128)
    group = jnp.dot((iota((CHIPS, CHIPS), 0) > iota((CHIPS, CHIPS), 1)).astype(F32), feeds_f).astype(I32)
    turn = jnp.dot(feeds_f, upper).astype(I32)
    place = ((turn & 7) << 7) + ((turn >> 3) << 5) + s_of
    both = jnp.where(feeds, (place << 6) + s_of, 0)
    rows = [jnp.sum(jnp.where(group == g, both, 0), axis=0, keepdims=True) for g in range(8)]
    both = jnp.concatenate(rows, axis=0)
    to_s, src = both >> 6, both & 63
    packed = jnp.where(feeds, turn * 8 + group + 1, 0).astype(F32)
    turned = jnp.transpose(jnp.concatenate([packed] * 4, axis=0)).astype(I32) - 1
    d_of, l_of = iota((128, 128), 0), iota((128, 128), 1)
    want = jnp.where(turned >= 0, (turned >> 3) - 8 * (l_of >> 5), -1)
    code = ((turned & 7) << 7) + d_of
    rows = [jnp.sum(jnp.where(want == q, code, 0), axis=0, keepdims=True) for q in range(8)]
    to_d = jnp.concatenate(rows, axis=0)

    row8, lane8 = iota((8, 128), 0), iota((8, 128), 1)
    here = (row8 << 7) + lane8

    def look(table, at):
        row, lane = at >> 7, at & 127
        out = jnp.zeros((8, 128), I32)
        for r in range(8):
            line = jnp.broadcast_to(table[r : r + 1, :], (8, 128))
            out = jnp.where(row == r, jnp.take_along_axis(line, lane, axis=1), out)
        return out

    def flip(x, k):
        for bit in (1, 2, 4):
            if k & bit:
                x = jnp.where((row8 & bit) == 0, pltpu.roll(x, 8 - bit, 0), pltpu.roll(x, bit, 0))
        return x

    def mate(x, colour, level):
        out = flip(x, level)
        for k in range(level + 1, 2 * level):
            out = jnp.where(flip(colour, k) == colour, flip(x, k), out)
        return out

    colour = jnp.zeros((8, 128), I32)
    for level, doublings in ((1, 8), (2, 7), (4, 6)):
        colour_s = look(colour, to_d) if level > 1 else colour
        partner = mate(here, colour_s, level)
        back = look(to_d, look(partner, to_s) if level > 1 else to_s ^ 128)
        hop = mate(back, colour, level)
        label = here
        for _ in range(doublings):
            got = look((hop << 10) + label, hop)
            label = jnp.minimum(label, got & 1023)
            hop = got >> 10
        colour = colour * 2 + (label > mate(label, colour, level)).astype(I32)

    colour_sd = jnp.zeros((CHIPS, 128), I32)
    colour_nd = jnp.zeros((NEW, 128), I32)
    for g in range(8):
        line, of = colour[g : g + 1, :], src[g : g + 1, :]
        colour_sd = colour_sd + jnp.where(s_of == of, line, 0)
        colour_nd = colour_nd + jnp.where(chip == of, line, 0)
    colour_sd = jnp.where(feeds, colour_sd, -1)
    masks = jnp.concatenate([(colour_sd == c).astype(F32) for c in range(8)], axis=0)
    counts = jnp.dot(masks, upper) * masks
    half = counts[0:CHIPS]
    for c in range(1, 8):
        half = half + counts[c * CHIPS : (c + 1) * CHIPS]
    half = half.astype(I32)
    own_chip = own >> 1
    mine = chip == own_chip
    slots = [
        jnp.sum(jnp.where(mine & (rank == r), local, 0), axis=0, keepdims=True) for r in range(4)
    ]
    slots = jnp.concatenate(slots + [jnp.zeros((4, 128), I32)], axis=0).astype(F32)
    own_row = s_of == own_chip
    colour_s = jnp.sum(jnp.where(own_row, colour_sd, 0), axis=0, keepdims=True)
    half_s = jnp.sum(jnp.where(own_row, half, 0), axis=0, keepdims=True)
    for h in range(2):
        pick = ((row8 == colour_s) & (half_s == h)).astype(F32)
        got = lax.dot_general(pick, slots, (((1,), (1,)), ((), ())), preferred_element_type=F32)
        out_ref[8 * h : 8 * h + 8, 0:8] = got.astype(I32)
    take = jnp.sum(jnp.where(colour_sd == own_chip >> 2, 2 * s_of + half, 0), axis=0, keepdims=True)
    out_ref[IDX2 : IDX2 + 8, :] = jnp.broadcast_to(take, (8, 128))
    via = colour_nd * 4 + rank
    via = jnp.sum(jnp.where(lane32 == own, via, 0), axis=1, keepdims=True)
    out_ref[IDX3 : IDX3 + NEW, :] = jnp.broadcast_to(via, (NEW, 128))


def matrices(cap_row, trans_row, out_ref):
    shape = (SH, 128)
    k_of, lane = iota(shape, 0), iota(shape, 1)
    eye = k_of == lane

    def column(row):
        return jnp.broadcast_to(jnp.sum(jnp.where(eye, row, 0.0), axis=1, keepdims=True), shape)

    cap, tr = column(cap_row), column(trans_row)
    inner = jnp.where(k_of == SH - 1, 0.0, pltpu.roll(tr, SH - 1, 0))
    t0 = jnp.broadcast_to(trans_row[:, 0:1], shape)
    b = cap + tr + inner
    c = -inner
    a = jnp.where(k_of == 0, 0.0, -tr)
    rhs = eye.astype(F32)
    s = 1
    while s < SH:
        up, down = (lambda x: pltpu.roll(x, s, 0)), (lambda x: pltpu.roll(x, SH - s, 0))
        al, ga = -a / up(b), -c / down(b)
        rhs = rhs + al * up(rhs) + ga * down(rhs)
        b = b + al * up(c) + ga * down(a)
        a, c = al * up(a), ga * down(c)
        s *= 2
    inverse = rhs / b
    amat = inverse * cap_row
    couple = jnp.broadcast_to(inverse[:, 0:1], shape) * t0
    asq = jnp.dot(amat[:, :SH], amat, precision=HI, preferred_element_type=F32)
    acouple = jnp.dot(amat[:, :SH], couple, precision=HI, preferred_element_type=F32)
    out_ref[0] = asq
    out_ref[1] = t0 * column(amat[0:1, :])
    out_ref[2] = t0 * column(asq[0:1, :])
    out_ref[3] = acouple
    out_ref[4] = couple
    out_ref[5, 0:8, :] = t0[0:8] * (1.0 - jnp.broadcast_to(couple[0:1], (8, 128)))
    out_ref[5, 8:16, :] = t0[0:8] * jnp.broadcast_to(acouple[0:1], (8, 128))


def prepare_kernel(own_of, tab_ref, cap_ref, trans_ref, tbl_ref, mat_ref):
    matrices(cap_ref[...], trans_ref[...], mat_ref)
    route(own_of(), tab_ref[...], tbl_ref)


def prepare(own_of, table, cap, tr, **more):
    tab = jnp.pad(table.reshape(SLABS, NEW).T, ((0, 0), (0, 128 - SLABS)), constant_values=-1)
    pad = lambda x: jnp.pad(x, (0, 128 - SH)).reshape(1, 128)
    return pl.pallas_call(
        functools.partial(prepare_kernel, own_of),
        out_shape=(jax.ShapeDtypeStruct((56, 128), I32), jax.ShapeDtypeStruct((6, SH, 128), F32)),
        in_specs=[pl.BlockSpec(memory_space=pltpu.VMEM)] * 3,
        out_specs=[pl.BlockSpec(memory_space=pltpu.VMEM)] * 2,
        **more,
    )(tab, pad(cap), pad(tr))


WIDE = 8
DEFAULTS = (1.0, 1.0, 0.0, 0.0, 0.0, 0.0, 0.0)
NF = len(DEFAULTS)
HALO = 2 * WIDE


def move_kernel(
    slabs, cols,
    tbl, p_ref, storage_ref, trans_ref, source_ref, old_ref, cb_ref, mat_ref,
    p_out, new_out,
    field, rows_in, edge_l, edge_r, from_l, from_r, line1, line2, shells1, shells2,
    stage1, mid, stage2, got, pb_stage, pb_mid,
    halo_send, halo_recv, send1, recv1, send_pb, recv_pb, send2, recv2,
):
    own, col = lax.axis_index("slab"), lax.axis_index("col")
    chip = own // 2
    first_core, second_core = own % 2 == 0, own % 2 == 1
    neighbours = []
    for dr, dc in ((-1, 0), (1, 0), (0, -1), (0, 1), (-1, -1), (1, -1), (-1, 1), (1, 1)):
        ok = None
        for step, at, size in ((dr, own, slabs), (dc, col, cols)):
            if step:
                inside = at > 0 if step < 0 else at < size - 1
                ok = inside if ok is None else ok & inside
        neighbours.append((ok, dr, dc))

    lane80 = iota((80, 128), 1)
    for f, value in enumerate(DEFAULTS):
        rows_in[f] = jnp.full((HALO, 256), value, F32)
    default = jnp.full((80, 128), 0.0, F32)
    for f, value in enumerate(DEFAULTS):
        if value:
            default = jnp.where(lane80 // WIDE == f, value, default)
    from_l[...] = default
    from_r[...] = default

    barrier = pltpu.get_barrier_semaphore()

    def greet(slab, c):
        pl.semaphore_signal(barrier, inc=1, device_id={"slab": slab, "col": c}, device_id_type=MESH)

    for ok, dr, dc in neighbours:
        if dc:
            @pl.when(ok)
            def _():
                greet(own + dr, col + dc)

    @pl.when(first_core)
    def _():
        def body(k, _):
            greet(2 * ((chip + k) % CHIPS) + 1, col)
            return 0
        lax.fori_loop(0, CHIPS, body, 0)

    @pl.when(second_core)
    def _():
        def body(k, _):
            greet((own + k) % slabs, col)
            return 0
        lax.fori_loop(1, slabs, body, 0)

    weight1, weight2 = mat_ref[1], mat_ref[2]

    @pl.when(first_core)
    def _():
        def body(o, _):
            x = old_ref[o]
            shells1[pl.ds(o, 1), :] = jnp.sum(x * weight1, axis=0, keepdims=True)
            shells2[pl.ds(o, 1), :] = jnp.sum(x * weight2, axis=0, keepdims=True)
            return 0
        lax.fori_loop(0, OLD, body, 0)

    row64 = iota((64, 64), 0)
    blocks = cb_ref[...]
    hot = [(blocks == 2 * row64 + h).astype(F32) for h in range(2)]
    field[0] = p_ref[...]
    field[1] = storage_ref[...]
    field[2] = trans_ref[...]
    field[3] = source_ref[...]

    @pl.when(first_core)
    def _():
        for h in range(2):
            part = pl.ds(128 * h, 128)
            field[4, :, part] = jnp.dot(hot[h], shells1[...], precision=HI, preferred_element_type=F32)
            field[5, :, part] = jnp.dot(hot[h], shells2[...], precision=HI, preferred_element_type=F32)
            field[6, :, part] = jnp.broadcast_to(jnp.sum(hot[h], axis=1, keepdims=True), (64, 128))

    @pl.when(second_core)
    def _():
        for f in range(4, 7):
            field[f] = jnp.zeros((64, 256), F32)

    lane64 = iota((64, 128), 1)
    left, right = jnp.zeros((64, 128), F32), jnp.zeros((64, 128), F32)
    for f in range(NF):
        spot = lane64 // WIDE == f
        a, b = field[f, :, 0:128], field[f, :, 128:256]
        left = jnp.where(spot, pltpu.roll(a, WIDE * f, 1) if f else a, left)
        right = jnp.where(spot, pltpu.roll(b, WIDE * (f + 1), 1), right)
    edge_l[...] = left
    edge_r[...] = right

    extra = (col > 0).astype(I32) + (col < cols - 1).astype(I32)
    near = 1 + (own > 0).astype(I32) + (own < slabs - 1).astype(I32)
    pl.semaphore_wait(barrier, extra * near + jnp.where(first_core, CHIPS, slabs - 1))

    def copy_of(i, dr, dc):
        if dc == 0:
            src = field.at[:, pl.ds(0 if dr < 0 else 64 - WIDE, WIDE), :]
            dst = rows_in.at[:, pl.ds(WIDE if dr > 0 else 0, WIDE), :]
        else:
            src, dst = (edge_l, from_r) if dc < 0 else (edge_r, from_l)
            if dr == 0:
                dst = dst.at[pl.ds(0, 64), :]
            else:
                src = src.at[pl.ds(0 if dr < 0 else 64 - WIDE, WIDE), :]
                dst = dst.at[pl.ds(64 + (WIDE if dr > 0 else 0), WIDE), :]
        return pltpu.make_async_remote_copy(
            src_ref=src, dst_ref=dst, send_sem=halo_send.at[i], recv_sem=halo_recv.at[i],
            device_id={"slab": own + dr, "col": col + dc}, device_id_type=MESH,
        )

    for i, (ok, dr, dc) in enumerate(neighbours):
        @pl.when(ok)
        def _():
            copy_of(i, dr, dc).start()

    def to_middle(src, dst, send, recv, m):
        return pltpu.make_async_remote_copy(
            src_ref=src, dst_ref=dst, send_sem=send, recv_sem=recv,
            device_id={"slab": 2 * m + 1}, device_id_type=MESH,
        )

    @pl.when(first_core)
    def _():
        square = mat_ref[0][:, :SH]

        def body(k, _):
            m = (chip + k) % CHIPS
            for h in range(2):
                slot = tbl[8 * h + m // 4, m % 4]
                stage1[2 * m + h] = jnp.dot(square, old_ref[slot], precision=HI, preferred_element_type=F32)
            to_middle(stage1.at[pl.ds(2 * m, 2)], mid.at[pl.ds(2 * chip, 2)], send1, recv1, m).start()
            return 0
        lax.fori_loop(0, CHIPS, body, 0)

    for i, (ok, dr, dc) in enumerate(neighbours):
        back = next(b for b, n in enumerate(neighbours) if n[1:] == (-dr, -dc))
        @pl.when(neighbours[back][0])
        def _():
            copy_of(i, dr, dc).wait_recv()

    shape = (64 + HALO, 384)
    in_l, in_r = from_l[...], from_r[...]

    def extended(f):
        rows = jnp.concatenate([field[f], rows_in[f]], axis=0)
        tail = jnp.where(lane80 >= 128 - WIDE, pltpu.roll(in_l, (128 - WIDE * (f + 1)) % 128, 1), DEFAULTS[f])
        tail = jnp.where(lane80 < WIDE, pltpu.roll(in_r, (128 - WIDE * f) % 128, 1), tail)
        return jnp.concatenate([rows, tail], axis=1)

    def after(x, axis):
        return pltpu.roll(x, shape[axis] - 1, axis)

    def before(x, axis):
        return pltpu.roll(x, 1, axis)

    p, storage, trans, source, base1, base2, active = [extended(f) for f in range(NF)]
    kappa, cross = mat_ref[5, 0:1, 0:1], mat_ref[5, 8:9, 0:1]
    faces = []
    for axis in (1, 0):
        other = after(trans, axis)
        total = trans + other
        faces.append(2.0 * trans * other / jnp.where(total == 0.0, 1.0, total))
    conduct = faces[0] + before(faces[0], 1) + faces[1] + before(faces[1], 0)
    draw = active * kappa
    slope0 = storage + draw
    half = [0.5 * x for x in faces]
    base = base1
    for step, line in ((0, line1), (1, line2)):
        prev = p
        for sweep in range(ITERS):
            if sweep == ITERS - 1:
                line[...] = p[0:64, 0:256]
                if step == 0:
                    base = base2 + active * (cross * p)
            flux = jnp.zeros(shape, F32)
            for axis, face in zip((1, 0), half):
                other = after(p, axis)
                flow = face * (other + p) * (other - p)
                flux = flux + flow - before(flow, axis)
            misfit = storage * (p - prev) - flux + (draw * p - (base1 if step == 0 else base)) - source
            p = p - misfit / (slope0 + p * conduct)
    p_out[...] = p[0:64, 0:256]

    @pl.when(first_core)
    def _():
        for line, rows in ((line1, shells1), (line2, shells2)):
            total = jnp.zeros((OLD, 128), F32)
            for h in range(2):
                total = total + lax.dot_general(
                    hot[h], line[:, 128 * h : 128 * h + 128], (((0,), (0,)), ((), ())),
                    precision=HI, preferred_element_type=F32,
                )
            rows[...] = total

        def body(k, _):
            m = (chip + k) % CHIPS
            for h in range(2):
                slot = tbl[8 * h + m // 4, m % 4]
                pb_stage[m, pl.ds(h, 1), :] = shells1[pl.ds(slot, 1), :]
                pb_stage[m, pl.ds(2 + h, 1), :] = shells2[pl.ds(slot, 1), :]
            for r in range(4, 8):
                pb_stage[m, pl.ds(r, 1), :] = jnp.zeros((1, 128), F32)
            to_middle(pb_stage.at[m], pb_mid.at[chip], send_pb, recv_pb, m).start()
            return 0
        lax.fori_loop(0, CHIPS, body, 0)

    def await_bytes(ref, sem):
        pltpu.make_async_copy(ref, ref, sem).wait()

    @pl.when(second_core)
    def _():
        await_bytes(mid, recv1)
        await_bytes(pb_mid, recv_pb)
        acouple, couple = mat_ref[3], mat_ref[4]

        def block(d):
            i = tbl[IDX2, d]
            s, h = i // 2, i % 2
            first = pb_mid[s, pl.ds(h, 1), :]
            second = pb_mid[s, pl.ds(2 + h, 1), :]
            return mid[i] + acouple * first + couple * second

        def body(k, _):
            d = (own + k) % slabs
            stage2[d] = block(d)
            pltpu.make_async_remote_copy(
                src_ref=stage2.at[d], dst_ref=got.at[chip], send_sem=send2, recv_sem=recv2,
                device_id={"slab": d}, device_id_type=MESH,
            ).start()
            return 0
        lax.fori_loop(1, slabs, body, 0)
        got[chip] = block(own)
        await_bytes(got.at[pl.ds(0, CHIPS - 1)], recv2)

    @pl.when(first_core)
    def _():
        await_bytes(got, recv2)

    def gather(n, _):
        new_out[n] = got[tbl[IDX3 + n, 0]]
        return 0
    lax.fori_loop(0, NEW, gather, 0)

    for i, (ok, dr, dc) in enumerate(neighbours):
        @pl.when(ok)
        def _():
            copy_of(i, dr, dc).wait_send()

    @pl.when(first_core)
    def _():
        await_bytes(stage1, send1)
        await_bytes(pb_stage, send_pb)

    @pl.when(second_core)
    def _():
        await_bytes(stage2.at[pl.ds(0, 2 * CHIPS - 1)], send2)


def solution(mesh):
    slabs, cols = mesh.shape["slab"], mesh.shape["col"]

    def shards(pressure, storage, trans, source, shells_old, cap, tr, new_source, cell_block):
        table, mats = prepare(lambda: lax.axis_index("slab"), new_source[0], cap, tr)
        vmem = pl.BlockSpec(memory_space=pltpu.VMEM)
        p, new = pl.pallas_call(
            functools.partial(move_kernel, slabs, cols),
            out_shape=(
                jax.ShapeDtypeStruct((64, 256), F32),
                jax.ShapeDtypeStruct((NEW, SH, 128), F32),
            ),
            in_specs=[pl.BlockSpec(memory_space=pltpu.SMEM)] + [vmem] * 7,
            out_specs=[vmem] * 2,
            scratch_shapes=[
                pltpu.VMEM((NF, 64, 256), F32),
                pltpu.VMEM((NF, HALO, 256), F32),
                pltpu.VMEM((64, 128), F32),
                pltpu.VMEM((64, 128), F32),
                pltpu.VMEM((80, 128), F32),
                pltpu.VMEM((80, 128), F32),
                pltpu.VMEM((64, 256), F32),
                pltpu.VMEM((64, 256), F32),
                pltpu.VMEM((OLD, 128), F32),
                pltpu.VMEM((OLD, 128), F32),
                pltpu.VMEM((2 * CHIPS, SH, 128), F32),
                pltpu.VMEM((2 * CHIPS, SH, 128), F32),
                pltpu.VMEM((2 * CHIPS, SH, 128), F32),
                pltpu.VMEM((CHIPS, SH, 128), F32),
                pltpu.VMEM((CHIPS, 8, 128), F32),
                pltpu.VMEM((CHIPS, 8, 128), F32),
                pltpu.SemaphoreType.DMA((8,)),
                pltpu.SemaphoreType.DMA((8,)),
            ] + [pltpu.SemaphoreType.DMA] * 6,
            compiler_params=pltpu.CompilerParams(
                collective_id=0, has_side_effects=True, vmem_limit_bytes=40 << 20
            ),
        )(table, pressure, storage, trans, source, shells_old[0], cell_block, mats)
        return p, new[None]

    f = P("slab", "col")
    return jax.shard_map(
        shards,
        mesh=mesh,
        in_specs=(f, f, f, f, P("col", "slab", None, None), P(), P(), P("col", None), P("col", "slab")),
        out_specs=(f, P("col", "slab", None, None)),
        check_vma=False,
    )
```

```python
import functools

import jax
import jax.numpy as jnp
from jax import lax
from jax.experimental import pallas as pl
from jax.experimental.pallas import tpu as pltpu
from jax.sharding import PartitionSpec as P

MESH = pl.DeviceIdType.MESH
HI = lax.Precision.HIGHEST
F32, I32 = jnp.float32, jnp.int32
SLABS = 64
CHIPS = 32
SH = 64
NEW = 32
OLD = 64
STEPS, ITERS = 2, 3
IDX2, IDX3 = 16, 24


def iota(shape, dim):
    return lax.broadcasted_iota(I32, shape, dim)


def strict_upper(n):
    return (iota((n, n), 0) < iota((n, n), 1)).astype(F32)


def lane_of(d):
    return (d & 3) * 16 + (d >> 2)


def by_owner(lines):
    turned = jnp.transpose(jnp.concatenate([lines.astype(F32)] * 8, axis=0)).astype(I32)
    part = iota((NEW, 128), 1) >> 4
    tab = jnp.full((NEW, 128), -1, I32)
    for a in range(4):
        tab = jnp.where(part == a, turned[NEW * a : NEW * a + NEW, :], tab)
    return tab


def route(own, tab, out_ref):
    chip, local = tab >> 7, tab & 63
    n_of, lane32 = iota((NEW, 128), 0), iota((NEW, 128), 1)
    rank = jnp.zeros((NEW, 128), I32)
    for k in range(1, NEW):
        rank = rank + ((pltpu.roll(chip, k, 0) == chip) & (n_of >= k)).astype(I32)
    s_of = n_of
    feeds = jnp.zeros((CHIPS, 128), jnp.bool_)
    for n in range(NEW):
        feeds = feeds | (s_of == chip[n : n + 1, :])
    feeds_f = feeds.astype(F32)
    upper = strict_upper(128)
    group = jnp.dot((iota((CHIPS, CHIPS), 0) > iota((CHIPS, CHIPS), 1)).astype(F32), feeds_f).astype(I32)
    turn = jnp.dot(feeds_f, upper).astype(I32)
    place = ((turn & 7) << 7) + ((turn >> 3) << 5) + s_of
    both = jnp.where(feeds, (place << 6) + s_of, 0)
    rows = [jnp.sum(jnp.where(group == g, both, 0), axis=0, keepdims=True) for g in range(8)]
    both = jnp.concatenate(rows, axis=0)
    to_s, src = both >> 6, both & 63
    packed = jnp.where(feeds, turn * 8 + group + 1, 0).astype(F32)
    turned = jnp.transpose(jnp.concatenate([packed] * 4, axis=0)).astype(I32) - 1
    d_of, l_of = iota((128, 128), 0), iota((128, 128), 1)
    want = jnp.where(turned >= 0, (turned >> 3) - 8 * (l_of >> 5), -1)
    code = ((turned & 7) << 7) + d_of
    rows = [jnp.sum(jnp.where(want == q, code, 0), axis=0, keepdims=True) for q in range(8)]
    to_d = jnp.concatenate(rows, axis=0)

    row8, lane8 = iota((8, 128), 0), iota((8, 128), 1)
    here = (row8 << 7) + lane8

    def look(table, at):
        row, lane = at >> 7, at & 127
        out = jnp.zeros((8, 128), I32)
        for r in range(8):
            line = jnp.broadcast_to(table[r : r + 1, :], (8, 128))
            out = jnp.where(row == r, jnp.take_along_axis(line, lane, axis=1), out)
        return out

    def flip(x, k):
        for bit in (1, 2, 4):
            if k & bit:
                x = jnp.where((row8 & bit) == 0, pltpu.roll(x, 8 - bit, 0), pltpu.roll(x, bit, 0))
        return x

    def mate(x, colour, level):
        out = flip(x, level)
        for k in range(level + 1, 2 * level):
            out = jnp.where(flip(colour, k) == colour, flip(x, k), out)
        return out

    colour = jnp.zeros((8, 128), I32)
    for level, doublings in ((1, 8), (2, 7), (4, 6)):
        colour_s = look(colour, to_d) if level > 1 else colour
        partner = mate(here, colour_s, level)
        back = look(to_d, look(partner, to_s) if level > 1 else to_s ^ 128)
        hop = mate(back, colour, level)
        label = here
        for _ in range(doublings):
            got = look((hop << 10) + label, hop)
            label = jnp.minimum(label, got & 1023)
            hop = got >> 10
        colour = colour * 2 + (label > mate(label, colour, level)).astype(I32)

    colour_sd = jnp.zeros((CHIPS, 128), I32)
    colour_nd = jnp.zeros((NEW, 128), I32)
    for g in range(8):
        line, of = colour[g : g + 1, :], src[g : g + 1, :]
        colour_sd = colour_sd + jnp.where(s_of == of, line, 0)
        colour_nd = colour_nd + jnp.where(chip == of, line, 0)
    colour_sd = jnp.where(feeds, colour_sd, -1)
    masks = jnp.concatenate([(colour_sd == c).astype(F32) for c in range(8)], axis=0)
    counts = jnp.dot(masks, upper) * masks
    half = counts[0:CHIPS]
    for c in range(1, 8):
        half = half + counts[c * CHIPS : (c + 1) * CHIPS]
    half = half.astype(I32)
    own_chip = own >> 1
    mine = chip == own_chip
    slots = [
        jnp.sum(jnp.where(mine & (rank == r), local, 0), axis=0, keepdims=True) for r in range(4)
    ]
    slots = jnp.concatenate(slots + [jnp.zeros((4, 128), I32)], axis=0).astype(F32)
    own_row = s_of == own_chip
    colour_s = jnp.sum(jnp.where(own_row, colour_sd, 0), axis=0, keepdims=True)
    half_s = jnp.sum(jnp.where(own_row, half, 0), axis=0, keepdims=True)
    for h in range(2):
        pick = ((row8 == colour_s) & (half_s == h)).astype(F32)
        got = lax.dot_general(pick, slots, (((1,), (1,)), ((), ())), preferred_element_type=F32)
        out_ref[8 * h : 8 * h + 8, 0:8] = got.astype(I32) & (OLD - 1)
    take = jnp.sum(jnp.where(colour_sd == own_chip >> 2, 2 * s_of + half, 0), axis=0, keepdims=True)
    out_ref[IDX2 : IDX2 + 8, :] = jnp.broadcast_to(take & (2 * CHIPS - 1), (8, 128))
    via = colour_nd * 4 + rank
    via = jnp.sum(jnp.where(lane32 == lane_of(own), via, 0), axis=1, keepdims=True)
    out_ref[IDX3 : IDX3 + NEW, :] = jnp.broadcast_to(via & (CHIPS - 1), (NEW, 128))


def matrices(cap_in, trans_in, out_ref):
    shape = (SH, 128)
    k_of, lane = iota(shape, 0), iota(shape, 1)
    eye = k_of == lane

    def column(row):
        square = iota((SH, SH), 0) == iota((SH, SH), 1)
        return jnp.broadcast_to(jnp.sum(jnp.where(square, row, 0.0), axis=1, keepdims=True), shape)

    cap, tr = column(cap_in), column(trans_in)
    cap_row = jnp.sum(jnp.where(eye, cap, 0.0), axis=0, keepdims=True)
    inner = jnp.where(k_of == SH - 1, 0.0, pltpu.roll(tr, SH - 1, 0))
    t0 = jnp.broadcast_to(tr[0:1, :], shape)
    b = cap + tr + inner
    c = -inner
    a = jnp.where(k_of == 0, 0.0, -tr)
    rhs = eye.astype(F32)
    s = 1
    while s < SH:
        up, down = (lambda x: pltpu.roll(x, s, 0)), (lambda x: pltpu.roll(x, SH - s, 0))
        al, ga = -a / up(b), -c / down(b)
        rhs = rhs + al * up(rhs) + ga * down(rhs)
        b = b + al * up(c) + ga * down(a)
        a, c = al * up(a), ga * down(c)
        s *= 2
    inverse = rhs / b
    amat = inverse * cap_row
    couple = jnp.broadcast_to(inverse[:, 0:1], shape) * t0
    asq = jnp.dot(amat[:, :SH], amat, precision=HI, preferred_element_type=F32)
    acouple = jnp.dot(amat[:, :SH], couple, precision=HI, preferred_element_type=F32)
    out_ref[0] = asq
    out_ref[1] = t0 * column(amat[0:1, :SH])
    out_ref[2] = t0 * column(asq[0:1, :SH])
    out_ref[3] = acouple
    out_ref[4] = couple
    out_ref[5, 0:8, :] = t0[0:8] * (1.0 - jnp.broadcast_to(couple[0:1], (8, 128)))
    out_ref[5, 8:16, :] = t0[0:8] * jnp.broadcast_to(acouple[0:1], (8, 128))


WIDE = 8
CHUNKS = 2
DEFAULTS = (1.0, 1.0, 0.0, 0.0, 0.0, 0.0, 0.0)
NF = len(DEFAULTS)
HALO = 2 * WIDE


def move_kernel(
    slabs, cols,
    table_hbm, cap_hbm, trans_row_hbm, cb_hbm, p_hbm, storage_hbm, trans_hbm, source_hbm, old_hbm,
    p_out, new_out,
    table_ref, cap_ref, trans_row_ref, cb_ref, old_ref, mat_ref, tbl_ref, tbl,
    field, rows_in, edge_l, edge_r, from_l, from_r, line1, line2, shells1, shells2,
    stage1, mid, stage2, got, pb_stage, pb_mid,
    load, load_old, load_tbl, halo_send, halo_recv, send1, recv1, send_pb, recv_pb, send2, recv2,
):
    own, col = lax.axis_index("slab"), lax.axis_index("col")
    chip = own // 2
    first_core, second_core = own % 2 == 0, own % 2 == 1
    loads = [
        pltpu.make_async_copy(src, dst, load.at[i])
        for i, (src, dst) in enumerate((
            (table_hbm, table_ref), (cap_hbm, cap_ref), (trans_row_hbm, trans_row_ref), (cb_hbm, cb_ref),
            (p_hbm, field.at[0]), (storage_hbm, field.at[1]), (trans_hbm, field.at[2]), (source_hbm, field.at[3]),
        ))
    ]
    old_load = pltpu.make_async_copy(old_hbm, old_ref, load_old)
    for one in loads:
        one.start()

    @pl.when(first_core)
    def _():
        old_load.start()

    neighbours = []
    for dr, dc in ((-1, 0), (1, 0), (0, -1), (0, 1), (-1, -1), (1, -1), (-1, 1), (1, 1)):
        ok = None
        for step, at, size in ((dr, own, slabs), (dc, col, cols)):
            if step:
                inside = at > 0 if step < 0 else at < size - 1
                ok = inside if ok is None else ok & inside
        neighbours.append((ok, dr, dc))

    lane80 = iota((80, 128), 1)
    for f, value in enumerate(DEFAULTS):
        rows_in[f] = jnp.full((HALO, 256), value, F32)
    default = jnp.full((80, 128), 0.0, F32)
    for f, value in enumerate(DEFAULTS):
        if value:
            default = jnp.where(lane80 // WIDE == f, value, default)
    from_l[...] = default
    from_r[...] = default

    barrier = pltpu.get_barrier_semaphore()

    def greet(slab, c):
        pl.semaphore_signal(barrier, inc=1, device_id={"slab": slab, "col": c}, device_id_type=MESH)

    for ok, dr, dc in neighbours:
        if dc:
            @pl.when(ok)
            def _():
                greet(own + dr, col + dc)

    @pl.when(first_core)
    def _():
        def body(k, _):
            greet(2 * ((chip + k) % CHIPS) + 1, col)
            return 0
        lax.fori_loop(0, CHIPS, body, 0)

    @pl.when(second_core)
    def _():
        def body(k, _):
            greet((own + k) % slabs, col)
            return 0
        lax.fori_loop(1, slabs, body, 0)

    for one in loads:
        one.wait()
    matrices(cap_ref[...], trans_row_ref[...], mat_ref)
    route(own, by_owner(table_ref[...]), tbl_ref)
    tbl_copy = pltpu.make_async_copy(tbl_ref, tbl, load_tbl)
    tbl_copy.start()

    weight1, weight2 = mat_ref[1], mat_ref[2]

    @pl.when(first_core)
    def _():
        old_load.wait()

        def body(o, _):
            first, second = [], []
            for j in range(8):
                x = old_ref[8 * o + j]
                first.append(jnp.sum(x * weight1, axis=0, keepdims=True))
                second.append(jnp.sum(x * weight2, axis=0, keepdims=True))
            shells1[pl.ds(8 * o, 8), :] = jnp.concatenate(first, axis=0)
            shells2[pl.ds(8 * o, 8), :] = jnp.concatenate(second, axis=0)
            return 0
        lax.fori_loop(0, OLD // 8, body, 0)

    row64 = iota((64, 64), 0)
    blocks = cb_ref[...]
    hot = [(blocks == 2 * row64 + h).astype(F32) for h in range(2)]

    @pl.when(first_core)
    def _():
        for h in range(2):
            part = pl.ds(128 * h, 128)
            field[4, :, part] = jnp.dot(hot[h], shells1[...], precision=HI, preferred_element_type=F32)
            field[5, :, part] = jnp.dot(hot[h], shells2[...], precision=HI, preferred_element_type=F32)
            field[6, :, part] = jnp.broadcast_to(jnp.sum(hot[h], axis=1, keepdims=True), (64, 128))

    @pl.when(second_core)
    def _():
        for f in range(4, 7):
            field[f] = jnp.zeros((64, 256), F32)

    lane64 = iota((64, 128), 1)
    left, right = jnp.zeros((64, 128), F32), jnp.zeros((64, 128), F32)
    for f in range(NF):
        spot = lane64 // WIDE == f
        a, b = field[f, :, 0:128], field[f, :, 128:256]
        left = jnp.where(spot, pltpu.roll(a, WIDE * f, 1) if f else a, left)
        right = jnp.where(spot, pltpu.roll(b, WIDE * (f + 1), 1), right)
    edge_l[...] = left
    edge_r[...] = right

    extra = (col > 0).astype(I32) + (col < cols - 1).astype(I32)
    near = 1 + (own > 0).astype(I32) + (own < slabs - 1).astype(I32)
    pl.semaphore_wait(barrier, extra * near + jnp.where(first_core, CHIPS, slabs - 1))

    def copy_of(i, dr, dc):
        if dc == 0:
            src = field.at[:, pl.ds(0 if dr < 0 else 64 - WIDE, WIDE), :]
            dst = rows_in.at[:, pl.ds(WIDE if dr > 0 else 0, WIDE), :]
        else:
            src, dst = (edge_l, from_r) if dc < 0 else (edge_r, from_l)
            if dr == 0:
                dst = dst.at[pl.ds(0, 64), :]
            else:
                src = src.at[pl.ds(0 if dr < 0 else 64 - WIDE, WIDE), :]
                dst = dst.at[pl.ds(64 + (WIDE if dr > 0 else 0), WIDE), :]
        return pltpu.make_async_remote_copy(
            src_ref=src, dst_ref=dst, send_sem=halo_send.at[i], recv_sem=halo_recv.at[i],
            device_id={"slab": own + dr, "col": col + dc}, device_id_type=MESH,
        )

    for i, (ok, dr, dc) in enumerate(neighbours):
        @pl.when(ok)
        def _():
            copy_of(i, dr, dc).start()

    def to_middle(src, dst, send, recv, m):
        return pltpu.make_async_remote_copy(
            src_ref=src, dst_ref=dst, send_sem=send, recv_sem=recv,
            device_id={"slab": 2 * m + 1}, device_id_type=MESH,
        )

    def rows_of(c):
        return pl.ds(SH // CHUNKS * c, SH // CHUNKS)

    def chunk_to_middle(c, m):
        src, dst = stage1.at[pl.ds(2 * m, 2), rows_of(c)], mid[c].at[pl.ds(2 * chip, 2)]
        to_middle(src, dst, send1.at[c], recv1.at[c], m).start()

    tbl_copy.wait()

    @pl.when(first_core)
    def _():
        square = mat_ref[0][:, :SH]

        def body(k, _):
            m = (chip + k) % CHIPS
            for h in range(2):
                slot = tbl[8 * h + m // 4, m % 4]
                stage1[2 * m + h] = jnp.dot(square, old_ref[slot], precision=HI, preferred_element_type=F32)
            chunk_to_middle(0, m)
            return 0
        lax.fori_loop(0, CHIPS, body, 0)

    for i, (ok, dr, dc) in enumerate(neighbours):
        back = next(b for b, n in enumerate(neighbours) if n[1:] == (-dr, -dc))
        @pl.when(neighbours[back][0])
        def _():
            copy_of(i, dr, dc).wait_recv()

    shape = (64 + HALO, 384)
    in_l, in_r = from_l[...], from_r[...]

    def extended(f):
        rows = jnp.concatenate([field[f], rows_in[f]], axis=0)
        tail = jnp.where(lane80 >= 128 - WIDE, pltpu.roll(in_l, (128 - WIDE * (f + 1)) % 128, 1), DEFAULTS[f])
        tail = jnp.where(lane80 < WIDE, pltpu.roll(in_r, (128 - WIDE * f) % 128, 1), tail)
        return jnp.concatenate([rows, tail], axis=1)

    def after(x, axis):
        return pltpu.roll(x, shape[axis] - 1, axis)

    def before(x, axis):
        return pltpu.roll(x, 1, axis)

    p, storage, trans, source, base1, base2, active = [extended(f) for f in range(NF)]
    kappa, cross = mat_ref[5, 0:1, 0:1], mat_ref[5, 8:9, 0:1]
    faces = []
    for axis in (1, 0):
        other = after(trans, axis)
        total = trans + other
        faces.append(2.0 * trans * other / jnp.where(total == 0.0, 1.0, total))
    conduct = faces[0] + before(faces[0], 1) + faces[1] + before(faces[1], 0)
    draw = active * kappa
    slope0 = storage + draw
    half = [0.5 * x for x in faces]
    base = base1
    for step, line in ((0, line1), (1, line2)):
        prev = p
        for sweep in range(ITERS):
            if sweep == ITERS - 1:
                line[...] = p[0:64, 0:256]
                if step == 0:
                    base = base2 + active * (cross * p)
            flux = jnp.zeros(shape, F32)
            for axis, face in zip((1, 0), half):
                other = after(p, axis)
                flow = face * (other + p) * (other - p)
                flux = flux + flow - before(flow, axis)
            misfit = storage * (p - prev) - flux + (draw * p - (base1 if step == 0 else base)) - source
            p = p - misfit / (slope0 + p * conduct)
    p_out[...] = p[0:64, 0:256]

    @pl.when(first_core)
    def _():
        for line, rows in ((line1, shells1), (line2, shells2)):
            total = jnp.zeros((OLD, 128), F32)
            for h in range(2):
                total = total + lax.dot_general(
                    hot[h], line[:, 128 * h : 128 * h + 128], (((0,), (0,)), ((), ())),
                    precision=HI, preferred_element_type=F32,
                )
            rows[...] = total

        def body(k, _):
            m = (chip + k) % CHIPS
            for h in range(2):
                slot = tbl[8 * h + m // 4, m % 4]
                pb_stage[m, pl.ds(h, 1), :] = shells1[pl.ds(slot, 1), :]
                pb_stage[m, pl.ds(2 + h, 1), :] = shells2[pl.ds(slot, 1), :]
            for r in range(4, 8):
                pb_stage[m, pl.ds(r, 1), :] = jnp.zeros((1, 128), F32)
            to_middle(pb_stage.at[m], pb_mid.at[chip], send_pb, recv_pb, m).start()
            return 0
        lax.fori_loop(0, CHIPS, body, 0)

        for c in range(1, CHUNKS):
            def later(k, _):
                chunk_to_middle(c, (chip + k) % CHIPS)
                return 0
            lax.fori_loop(0, CHIPS, later, 0)

    def await_bytes(ref, sem):
        pltpu.make_async_copy(ref, ref, sem).wait()

    @pl.when(second_core)
    def _():
        for c in range(CHUNKS):
            rows = rows_of(c)
            await_bytes(mid[c], recv1.at[c])
            if c == 0:
                await_bytes(pb_mid, recv_pb)
            acouple, couple = mat_ref[3, rows], mat_ref[4, rows]

            def block(d):
                i = tbl[IDX2, lane_of(d)]
                s, h = i // 2, i % 2
                first = pb_mid[s, pl.ds(h, 1), :]
                second = pb_mid[s, pl.ds(2 + h, 1), :]
                return mid[c][i] + acouple * first + couple * second

            def body(k, _):
                d = (own + k) % slabs
                stage2[d, rows] = block(d)
                pltpu.make_async_remote_copy(
                    src_ref=stage2.at[d, rows], dst_ref=got.at[chip, rows], send_sem=send2.at[c], recv_sem=recv2.at[c],
                    device_id={"slab": d}, device_id_type=MESH,
                ).start()
                return 0
            lax.fori_loop(1, slabs, body, 0)
            got[chip, rows] = block(own)
        for c in range(CHUNKS):
            await_bytes(got.at[pl.ds(0, CHIPS - 1), rows_of(c)], recv2.at[c])

    @pl.when(first_core)
    def _():
        for c in range(CHUNKS):
            await_bytes(got.at[:, rows_of(c)], recv2.at[c])

    def gather(n, _):
        new_out[n] = got[tbl[IDX3 + n, 0]]
        return 0
    lax.fori_loop(0, NEW, gather, 0)

    for i, (ok, dr, dc) in enumerate(neighbours):
        @pl.when(ok)
        def _():
            copy_of(i, dr, dc).wait_send()

    @pl.when(first_core)
    def _():
        for c in range(CHUNKS):
            await_bytes(stage1.at[:, rows_of(c)], send1.at[c])
        await_bytes(pb_stage, send_pb)

    @pl.when(second_core)
    def _():
        for c in range(CHUNKS):
            await_bytes(stage2.at[pl.ds(0, 2 * CHIPS - 1), rows_of(c)], send2.at[c])


def solution(mesh):
    slabs, cols = mesh.shape["slab"], mesh.shape["col"]

    def shards(pressure, storage, trans, source, shells_old, cap, tr, new_source, cell_block):
        vmem = pl.BlockSpec(memory_space=pltpu.VMEM)
        p, new = pl.pallas_call(
            functools.partial(move_kernel, slabs, cols),
            out_shape=(
                jax.ShapeDtypeStruct((64, 256), F32),
                jax.ShapeDtypeStruct((NEW, SH, 128), F32),
            ),
            in_specs=[pl.BlockSpec(memory_space=pl.ANY)] * 9,
            out_specs=[vmem] * 2,
            scratch_shapes=[
                pltpu.VMEM((16, 128), I32),
                pltpu.VMEM((1, SH), F32),
                pltpu.VMEM((1, SH), F32),
                pltpu.VMEM((1, OLD), I32),
                pltpu.VMEM((OLD, SH, 128), F32),
                pltpu.VMEM((6, SH, 128), F32),
                pltpu.VMEM((56, 128), I32),
                pltpu.SMEM((56, 128), I32),
                pltpu.VMEM((NF, 64, 256), F32),
                pltpu.VMEM((NF, HALO, 256), F32),
                pltpu.VMEM((64, 128), F32),
                pltpu.VMEM((64, 128), F32),
                pltpu.VMEM((80, 128), F32),
                pltpu.VMEM((80, 128), F32),
                pltpu.VMEM((64, 256), F32),
                pltpu.VMEM((64, 256), F32),
                pltpu.VMEM((OLD, 128), F32),
                pltpu.VMEM((OLD, 128), F32),
                pltpu.VMEM((2 * CHIPS, SH, 128), F32),
                tuple(pltpu.VMEM((2 * CHIPS, SH // CHUNKS, 128), F32) for _ in range(CHUNKS)),
                pltpu.VMEM((2 * CHIPS, SH, 128), F32),
                pltpu.VMEM((CHIPS, SH, 128), F32),
                pltpu.VMEM((CHIPS, 8, 128), F32),
                pltpu.VMEM((CHIPS, 8, 128), F32),
                pltpu.SemaphoreType.DMA((8,)),
                pltpu.SemaphoreType.DMA,
                pltpu.SemaphoreType.DMA,
                pltpu.SemaphoreType.DMA((8,)),
                pltpu.SemaphoreType.DMA((8,)),
                pltpu.SemaphoreType.DMA((CHUNKS,)),
                pltpu.SemaphoreType.DMA((CHUNKS,)),
                pltpu.SemaphoreType.DMA,
                pltpu.SemaphoreType.DMA,
                pltpu.SemaphoreType.DMA((CHUNKS,)),
                pltpu.SemaphoreType.DMA((CHUNKS,)),
            ],
            compiler_params=pltpu.CompilerParams(
                collective_id=0, has_side_effects=True, vmem_limit_bytes=60 << 20
            ),
        )(
            new_source.reshape(16, 128), cap.reshape(1, SH), tr.reshape(1, SH), cell_block,
            pressure, storage, trans, source, shells_old[0],
        )
        return p, new[None]

    f = P("slab", "col")
    return jax.shard_map(
        shards,
        mesh=mesh,
        in_specs=(f, f, f, f, P("col", "slab", None, None), P(), P(), P("col", None), P("col", "slab")),
        out_specs=(f, P("col", "slab", None, None)),
        check_vma=False,
    )
```

```python
import functools

import jax
import jax.numpy as jnp
from jax import lax
from jax.experimental import pallas as pl
from jax.experimental.pallas import tpu as pltpu
from jax.sharding import PartitionSpec as P

MESH = pl.DeviceIdType.MESH
HI = lax.Precision.HIGHEST
F32, I32 = jnp.float32, jnp.int32
SLABS = 64
CHIPS = 32
SH = 64
NEW = 32
OLD = 64
STEPS, ITERS = 2, 3
IDX2, IDX3 = 16, 24


def iota(shape, dim):
    return lax.broadcasted_iota(I32, shape, dim)


def strict_upper(n):
    return (iota((n, n), 0) < iota((n, n), 1)).astype(F32)


def lane_of(d):
    return (d & 3) * 16 + (d >> 2)


def by_owner(lines):
    turned = jnp.transpose(jnp.concatenate([lines.astype(F32)] * 8, axis=0)).astype(I32)
    part = iota((NEW, 128), 1) >> 4
    tab = jnp.full((NEW, 128), -1, I32)
    for a in range(4):
        tab = jnp.where(part == a, turned[NEW * a : NEW * a + NEW, :], tab)
    return tab


def route(own, tab, out_ref):
    chip, local = tab >> 7, tab & 63
    n_of, lane32 = iota((NEW, 128), 0), iota((NEW, 128), 1)
    rank = jnp.zeros((NEW, 128), I32)
    for k in range(1, NEW):
        rank = rank + ((pltpu.roll(chip, k, 0) == chip) & (n_of >= k)).astype(I32)
    s_of = n_of
    feeds = jnp.zeros((CHIPS, 128), jnp.bool_)
    for n in range(NEW):
        feeds = feeds | (s_of == chip[n : n + 1, :])
    feeds_f = feeds.astype(F32)
    upper = strict_upper(128)
    group = jnp.dot((iota((CHIPS, CHIPS), 0) > iota((CHIPS, CHIPS), 1)).astype(F32), feeds_f).astype(I32)
    turn = jnp.dot(feeds_f, upper).astype(I32)
    place = ((turn & 7) << 7) + ((turn >> 3) << 5) + s_of
    both = jnp.where(feeds, (place << 6) + s_of, 0)
    rows = [jnp.sum(jnp.where(group == g, both, 0), axis=0, keepdims=True) for g in range(8)]
    both = jnp.concatenate(rows, axis=0)
    to_s, src = both >> 6, both & 63
    packed = jnp.where(feeds, turn * 8 + group + 1, 0).astype(F32)
    turned = jnp.transpose(jnp.concatenate([packed] * 4, axis=0)).astype(I32) - 1
    d_of, l_of = iota((128, 128), 0), iota((128, 128), 1)
    want = jnp.where(turned >= 0, (turned >> 3) - 8 * (l_of >> 5), -1)
    code = ((turned & 7) << 7) + d_of
    rows = [jnp.sum(jnp.where(want == q, code, 0), axis=0, keepdims=True) for q in range(8)]
    to_d = jnp.concatenate(rows, axis=0)

    row8, lane8 = iota((8, 128), 0), iota((8, 128), 1)
    here = (row8 << 7) + lane8

    def look(table, at):
        row, lane = at >> 7, at & 127
        out = jnp.zeros((8, 128), I32)
        for r in range(8):
            line = jnp.broadcast_to(table[r : r + 1, :], (8, 128))
            out = jnp.where(row == r, jnp.take_along_axis(line, lane, axis=1), out)
        return out

    def flip(x, k):
        for bit in (1, 2, 4):
            if k & bit:
                x = jnp.where((row8 & bit) == 0, pltpu.roll(x, 8 - bit, 0), pltpu.roll(x, bit, 0))
        return x

    def mate(x, colour, level):
        out = flip(x, level)
        for k in range(level + 1, 2 * level):
            out = jnp.where(flip(colour, k) == colour, flip(x, k), out)
        return out

    colour = jnp.zeros((8, 128), I32)
    for level, doublings in ((1, 8), (2, 7), (4, 6)):
        colour_s = look(colour, to_d) if level > 1 else colour
        partner = mate(here, colour_s, level)
        back = look(to_d, look(partner, to_s) if level > 1 else to_s ^ 128)
        hop = mate(back, colour, level)
        label = here
        for _ in range(doublings):
            got = look((hop << 10) + label, hop)
            label = jnp.minimum(label, got & 1023)
            hop = got >> 10
        colour = colour * 2 + (label > mate(label, colour, level)).astype(I32)

    colour_sd = jnp.zeros((CHIPS, 128), I32)
    colour_nd = jnp.zeros((NEW, 128), I32)
    for g in range(8):
        line, of = colour[g : g + 1, :], src[g : g + 1, :]
        colour_sd = colour_sd + jnp.where(s_of == of, line, 0)
        colour_nd = colour_nd + jnp.where(chip == of, line, 0)
    colour_sd = jnp.where(feeds, colour_sd, -1)
    masks = jnp.concatenate([(colour_sd == c).astype(F32) for c in range(8)], axis=0)
    counts = jnp.dot(masks, upper) * masks
    half = counts[0:CHIPS]
    for c in range(1, 8):
        half = half + counts[c * CHIPS : (c + 1) * CHIPS]
    half = half.astype(I32)
    own_chip = own >> 1
    mine = chip == own_chip
    slots = [
        jnp.sum(jnp.where(mine & (rank == r), local, 0), axis=0, keepdims=True) for r in range(4)
    ]
    slots = jnp.concatenate(slots + [jnp.zeros((4, 128), I32)], axis=0).astype(F32)
    own_row = s_of == own_chip
    colour_s = jnp.sum(jnp.where(own_row, colour_sd, 0), axis=0, keepdims=True)
    half_s = jnp.sum(jnp.where(own_row, half, 0), axis=0, keepdims=True)
    for h in range(2):
        pick = ((row8 == colour_s) & (half_s == h)).astype(F32)
        got = lax.dot_general(pick, slots, (((1,), (1,)), ((), ())), preferred_element_type=F32)
        out_ref[8 * h : 8 * h + 8, 0:8] = got.astype(I32) & (OLD - 1)
    take = jnp.sum(jnp.where(colour_sd == own_chip >> 2, 2 * s_of + half, 0), axis=0, keepdims=True)
    out_ref[IDX2 : IDX2 + 8, :] = jnp.broadcast_to(take & (2 * CHIPS - 1), (8, 128))
    via = colour_nd * 4 + rank
    via = jnp.sum(jnp.where(lane32 == lane_of(own), via, 0), axis=1, keepdims=True)
    out_ref[IDX3 : IDX3 + NEW, :] = jnp.broadcast_to(via & (CHIPS - 1), (NEW, 128))


def matrices(cap_in, trans_in, out_ref):
    shape = (SH, 128)
    k_of, lane = iota(shape, 0), iota(shape, 1)
    eye = k_of == lane

    def column(row):
        square = iota((SH, SH), 0) == iota((SH, SH), 1)
        return jnp.broadcast_to(jnp.sum(jnp.where(square, row, 0.0), axis=1, keepdims=True), shape)

    cap, tr = column(cap_in), column(trans_in)
    cap_row = jnp.sum(jnp.where(eye, cap, 0.0), axis=0, keepdims=True)
    inner = jnp.where(k_of == SH - 1, 0.0, pltpu.roll(tr, SH - 1, 0))
    t0 = jnp.broadcast_to(tr[0:1, :], shape)
    b = cap + tr + inner
    c = -inner
    a = jnp.where(k_of == 0, 0.0, -tr)
    rhs = eye.astype(F32)
    s = 1
    while s < SH:
        up, down = (lambda x: pltpu.roll(x, s, 0)), (lambda x: pltpu.roll(x, SH - s, 0))
        al, ga = -a / up(b), -c / down(b)
        rhs = rhs + al * up(rhs) + ga * down(rhs)
        b = b + al * up(c) + ga * down(a)
        a, c = al * up(a), ga * down(c)
        s *= 2
    inverse = rhs / b
    amat = inverse * cap_row
    couple = jnp.broadcast_to(inverse[:, 0:1], shape) * t0
    asq = jnp.dot(amat[:, :SH], amat, precision=HI, preferred_element_type=F32)
    acouple = jnp.dot(amat[:, :SH], couple, precision=HI, preferred_element_type=F32)
    out_ref[0] = asq
    out_ref[1] = t0 * column(amat[0:1, :SH])
    out_ref[2] = t0 * column(asq[0:1, :SH])
    out_ref[3] = acouple
    out_ref[4] = couple
    out_ref[5, 0:8, :] = t0[0:8] * (1.0 - jnp.broadcast_to(couple[0:1], (8, 128)))
    out_ref[5, 8:16, :] = t0[0:8] * jnp.broadcast_to(acouple[0:1], (8, 128))


WIDE = 8
PARTS = (40, 24)
CHUNKS = len(PARTS)
DEFAULTS = (1.0, 1.0, 0.0, 0.0, 0.0, 0.0, 0.0)
NF = len(DEFAULTS)
HALO = 2 * WIDE


def move_kernel(
    slabs, cols,
    table_hbm, cap_hbm, trans_row_hbm, cb_hbm, p_hbm, storage_hbm, trans_hbm, source_hbm, old_hbm,
    p_out, new_out,
    table_ref, cap_ref, trans_row_ref, cb_ref, old_ref, mat_ref, tbl_ref, tbl,
    field, rows_in, edge_l, edge_r, from_l, from_r, line1, line2, shells1, shells2,
    stage1, mid, stage2, got, pb_stage, pb_mid,
    load, load_old, load_tbl, halo_send, halo_recv, send1, recv1, send_pb, recv_pb, send2, recv2,
):
    own, col = lax.axis_index("slab"), lax.axis_index("col")
    chip = own // 2
    first_core, second_core = own % 2 == 0, own % 2 == 1
    loads = [
        pltpu.make_async_copy(src, dst, load.at[i])
        for i, (src, dst) in enumerate((
            (table_hbm, table_ref), (cap_hbm, cap_ref), (trans_row_hbm, trans_row_ref), (cb_hbm, cb_ref),
            (p_hbm, field.at[0]), (storage_hbm, field.at[1]), (trans_hbm, field.at[2]), (source_hbm, field.at[3]),
        ))
    ]
    old_load = pltpu.make_async_copy(old_hbm, old_ref, load_old)
    for one in loads:
        one.start()

    @pl.when(first_core)
    def _():
        old_load.start()

    neighbours = []
    for dr, dc in ((-1, 0), (1, 0), (0, -1), (0, 1), (-1, -1), (1, -1), (-1, 1), (1, 1)):
        ok = None
        for step, at, size in ((dr, own, slabs), (dc, col, cols)):
            if step:
                inside = at > 0 if step < 0 else at < size - 1
                ok = inside if ok is None else ok & inside
        neighbours.append((ok, dr, dc))

    lane80 = iota((80, 128), 1)
    for f, value in enumerate(DEFAULTS):
        rows_in[f] = jnp.full((HALO, 256), value, F32)
    default = jnp.full((80, 128), 0.0, F32)
    for f, value in enumerate(DEFAULTS):
        if value:
            default = jnp.where(lane80 // WIDE == f, value, default)
    from_l[...] = default
    from_r[...] = default

    barrier = pltpu.get_barrier_semaphore()

    def greet(slab, c):
        pl.semaphore_signal(barrier, inc=1, device_id={"slab": slab, "col": c}, device_id_type=MESH)

    for ok, dr, dc in neighbours:
        if dc:
            @pl.when(ok)
            def _():
                greet(own + dr, col + dc)

    @pl.when(first_core)
    def _():
        def body(k, _):
            greet(2 * ((chip + k) % CHIPS) + 1, col)
            return 0
        lax.fori_loop(0, CHIPS, body, 0)

    @pl.when(second_core)
    def _():
        def body(k, _):
            greet((own + k) % slabs, col)
            return 0
        lax.fori_loop(1, slabs, body, 0)

    for one in loads:
        one.wait()
    matrices(cap_ref[...], trans_row_ref[...], mat_ref)
    route(own, by_owner(table_ref[...]), tbl_ref)
    tbl_copy = pltpu.make_async_copy(tbl_ref, tbl, load_tbl)
    tbl_copy.start()

    weight1, weight2 = mat_ref[1], mat_ref[2]

    @pl.when(first_core)
    def _():
        old_load.wait()

        def body(o, _):
            first, second = [], []
            for j in range(8):
                x = old_ref[8 * o + j]
                first.append(jnp.sum(x * weight1, axis=0, keepdims=True))
                second.append(jnp.sum(x * weight2, axis=0, keepdims=True))
            shells1[pl.ds(8 * o, 8), :] = jnp.concatenate(first, axis=0)
            shells2[pl.ds(8 * o, 8), :] = jnp.concatenate(second, axis=0)
            return 0
        lax.fori_loop(0, OLD // 8, body, 0)

    row64 = iota((64, 64), 0)
    blocks = cb_ref[...]
    hot = [(blocks == 2 * row64 + h).astype(F32) for h in range(2)]

    @pl.when(first_core)
    def _():
        for h in range(2):
            part = pl.ds(128 * h, 128)
            field[4, :, part] = jnp.dot(hot[h], shells1[...], precision=HI, preferred_element_type=F32)
            field[5, :, part] = jnp.dot(hot[h], shells2[...], precision=HI, preferred_element_type=F32)
            field[6, :, part] = jnp.broadcast_to(jnp.sum(hot[h], axis=1, keepdims=True), (64, 128))

    @pl.when(second_core)
    def _():
        for f in range(4, 7):
            field[f] = jnp.zeros((64, 256), F32)

    lane64 = iota((64, 128), 1)
    left, right = jnp.zeros((64, 128), F32), jnp.zeros((64, 128), F32)
    for f in range(NF):
        spot = lane64 // WIDE == f
        a, b = field[f, :, 0:128], field[f, :, 128:256]
        left = jnp.where(spot, pltpu.roll(a, WIDE * f, 1) if f else a, left)
        right = jnp.where(spot, pltpu.roll(b, WIDE * (f + 1), 1), right)
    edge_l[...] = left
    edge_r[...] = right

    extra = (col > 0).astype(I32) + (col < cols - 1).astype(I32)
    near = 1 + (own > 0).astype(I32) + (own < slabs - 1).astype(I32)
    pl.semaphore_wait(barrier, extra * near + jnp.where(first_core, CHIPS, slabs - 1))

    def copy_of(i, dr, dc):
        if dc == 0:
            src = field.at[:, pl.ds(0 if dr < 0 else 64 - WIDE, WIDE), :]
            dst = rows_in.at[:, pl.ds(WIDE if dr > 0 else 0, WIDE), :]
        else:
            src, dst = (edge_l, from_r) if dc < 0 else (edge_r, from_l)
            if dr == 0:
                dst = dst.at[pl.ds(0, 64), :]
            else:
                src = src.at[pl.ds(0 if dr < 0 else 64 - WIDE, WIDE), :]
                dst = dst.at[pl.ds(64 + (WIDE if dr > 0 else 0), WIDE), :]
        return pltpu.make_async_remote_copy(
            src_ref=src, dst_ref=dst, send_sem=halo_send.at[i], recv_sem=halo_recv.at[i],
            device_id={"slab": own + dr, "col": col + dc}, device_id_type=MESH,
        )

    for i, (ok, dr, dc) in enumerate(neighbours):
        @pl.when(ok)
        def _():
            copy_of(i, dr, dc).start()

    def to_middle(src, dst, send, recv, m):
        return pltpu.make_async_remote_copy(
            src_ref=src, dst_ref=dst, send_sem=send, recv_sem=recv,
            device_id={"slab": 2 * m + 1}, device_id_type=MESH,
        )

    def rows_of(c):
        return pl.ds(sum(PARTS[:c]), PARTS[c])

    def chunk_to_middle(c, m):
        src, dst = stage1.at[pl.ds(2 * m, 2), rows_of(c)], mid[c].at[pl.ds(2 * chip, 2)]
        to_middle(src, dst, send1.at[c], recv1.at[c], m).start()

    tbl_copy.wait()

    @pl.when(first_core)
    def _():
        square = mat_ref[0][:, :SH]

        def body(k, _):
            m = (chip + k) % CHIPS
            for h in range(2):
                slot = tbl[8 * h + m // 4, m % 4]
                stage1[2 * m + h] = jnp.dot(square, old_ref[slot], precision=HI, preferred_element_type=F32)
            chunk_to_middle(0, m)
            return 0
        lax.fori_loop(0, CHIPS, body, 0)

    for i, (ok, dr, dc) in enumerate(neighbours):
        back = next(b for b, n in enumerate(neighbours) if n[1:] == (-dr, -dc))
        @pl.when(neighbours[back][0])
        def _():
            copy_of(i, dr, dc).wait_recv()

    shape = (64 + HALO, 384)
    in_l, in_r = from_l[...], from_r[...]

    def extended(f):
        rows = jnp.concatenate([field[f], rows_in[f]], axis=0)
        tail = jnp.where(lane80 >= 128 - WIDE, pltpu.roll(in_l, (128 - WIDE * (f + 1)) % 128, 1), DEFAULTS[f])
        tail = jnp.where(lane80 < WIDE, pltpu.roll(in_r, (128 - WIDE * f) % 128, 1), tail)
        return jnp.concatenate([rows, tail], axis=1)

    def after(x, axis):
        return pltpu.roll(x, shape[axis] - 1, axis)

    def before(x, axis):
        return pltpu.roll(x, 1, axis)

    p, storage, trans, source, base1, base2, active = [extended(f) for f in range(NF)]
    kappa, cross = mat_ref[5, 0:1, 0:1], mat_ref[5, 8:9, 0:1]
    faces = []
    for axis in (1, 0):
        other = after(trans, axis)
        total = trans + other
        faces.append(2.0 * trans * other / jnp.where(total == 0.0, 1.0, total))
    conduct = faces[0] + before(faces[0], 1) + faces[1] + before(faces[1], 0)
    draw = active * kappa
    slope0 = storage + draw
    half = [0.5 * x for x in faces]
    base = base1
    for step, line in ((0, line1), (1, line2)):
        prev = p
        for sweep in range(ITERS):
            if sweep == ITERS - 1:
                line[...] = p[0:64, 0:256]
                if step == 0:
                    base = base2 + active * (cross * p)
            flux = jnp.zeros(shape, F32)
            for axis, face in zip((1, 0), half):
                other = after(p, axis)
                flow = face * (other + p) * (other - p)
                flux = flux + flow - before(flow, axis)
            misfit = storage * (p - prev) - flux + (draw * p - (base1 if step == 0 else base)) - source
            p = p - misfit / (slope0 + p * conduct)
    p_out[...] = p[0:64, 0:256]

    @pl.when(first_core)
    def _():
        for line, rows in ((line1, shells1), (line2, shells2)):
            total = jnp.zeros((OLD, 128), F32)
            for h in range(2):
                total = total + lax.dot_general(
                    hot[h], line[:, 128 * h : 128 * h + 128], (((0,), (0,)), ((), ())),
                    precision=HI, preferred_element_type=F32,
                )
            rows[...] = total

        def body(k, _):
            m = (chip + k) % CHIPS
            for h in range(2):
                slot = tbl[8 * h + m // 4, m % 4]
                pb_stage[m, pl.ds(h, 1), :] = shells1[pl.ds(slot, 1), :]
                pb_stage[m, pl.ds(2 + h, 1), :] = shells2[pl.ds(slot, 1), :]
            for r in range(4, 8):
                pb_stage[m, pl.ds(r, 1), :] = jnp.zeros((1, 128), F32)
            to_middle(pb_stage.at[m], pb_mid.at[chip], send_pb, recv_pb, m).start()
            return 0
        lax.fori_loop(0, CHIPS, body, 0)

        for c in range(1, CHUNKS):
            def later(k, _):
                chunk_to_middle(c, (chip + k) % CHIPS)
                return 0
            lax.fori_loop(0, CHIPS, later, 0)

    def await_bytes(ref, sem):
        pltpu.make_async_copy(ref, ref, sem).wait()

    @pl.when(second_core)
    def _():
        for c in range(CHUNKS):
            rows = rows_of(c)
            await_bytes(mid[c], recv1.at[c])
            if c == 0:
                await_bytes(pb_mid, recv_pb)
            acouple, couple = mat_ref[3, rows], mat_ref[4, rows]

            def block(d):
                i = tbl[IDX2, lane_of(d)]
                s, h = i // 2, i % 2
                first = pb_mid[s, pl.ds(h, 1), :]
                second = pb_mid[s, pl.ds(2 + h, 1), :]
                return mid[c][i] + acouple * first + couple * second

            def body(k, _):
                d = (own + k) % slabs
                stage2[d, rows] = block(d)
                pltpu.make_async_remote_copy(
                    src_ref=stage2.at[d, rows], dst_ref=got.at[chip, rows], send_sem=send2.at[c], recv_sem=recv2.at[c],
                    device_id={"slab": d}, device_id_type=MESH,
                ).start()
                return 0
            lax.fori_loop(1, slabs, body, 0)
            got[chip, rows] = block(own)
        for c in range(CHUNKS):
            await_bytes(got.at[pl.ds(0, CHIPS - 1), rows_of(c)], recv2.at[c])

    @pl.when(first_core)
    def _():
        for c in range(CHUNKS):
            await_bytes(got.at[:, rows_of(c)], recv2.at[c])

    def gather(n, _):
        new_out[n] = got[tbl[IDX3 + n, 0]]
        return 0
    lax.fori_loop(0, NEW, gather, 0)

    for i, (ok, dr, dc) in enumerate(neighbours):
        @pl.when(ok)
        def _():
            copy_of(i, dr, dc).wait_send()

    @pl.when(first_core)
    def _():
        for c in range(CHUNKS):
            await_bytes(stage1.at[:, rows_of(c)], send1.at[c])
        await_bytes(pb_stage, send_pb)

    @pl.when(second_core)
    def _():
        for c in range(CHUNKS):
            await_bytes(stage2.at[pl.ds(0, 2 * CHIPS - 1), rows_of(c)], send2.at[c])


def solution(mesh):
    slabs, cols = mesh.shape["slab"], mesh.shape["col"]

    def shards(pressure, storage, trans, source, shells_old, cap, tr, new_source, cell_block):
        vmem = pl.BlockSpec(memory_space=pltpu.VMEM)
        p, new = pl.pallas_call(
            functools.partial(move_kernel, slabs, cols),
            out_shape=(
                jax.ShapeDtypeStruct((64, 256), F32),
                jax.ShapeDtypeStruct((NEW, SH, 128), F32),
            ),
            in_specs=[pl.BlockSpec(memory_space=pl.ANY)] * 9,
            out_specs=[vmem] * 2,
            scratch_shapes=[
                pltpu.VMEM((16, 128), I32),
                pltpu.VMEM((1, SH), F32),
                pltpu.VMEM((1, SH), F32),
                pltpu.VMEM((1, OLD), I32),
                pltpu.VMEM((OLD, SH, 128), F32),
                pltpu.VMEM((6, SH, 128), F32),
                pltpu.VMEM((56, 128), I32),
                pltpu.SMEM((56, 128), I32),
                pltpu.VMEM((NF, 64, 256), F32),
                pltpu.VMEM((NF, HALO, 256), F32),
                pltpu.VMEM((64, 128), F32),
                pltpu.VMEM((64, 128), F32),
                pltpu.VMEM((80, 128), F32),
                pltpu.VMEM((80, 128), F32),
                pltpu.VMEM((64, 256), F32),
                pltpu.VMEM((64, 256), F32),
                pltpu.VMEM((OLD, 128), F32),
                pltpu.VMEM((OLD, 128), F32),
                pltpu.VMEM((2 * CHIPS, SH, 128), F32),
                tuple(pltpu.VMEM((2 * CHIPS, part, 128), F32) for part in PARTS),
                pltpu.VMEM((2 * CHIPS, SH, 128), F32),
                pltpu.VMEM((CHIPS, SH, 128), F32),
                pltpu.VMEM((CHIPS, 8, 128), F32),
                pltpu.VMEM((CHIPS, 8, 128), F32),
                pltpu.SemaphoreType.DMA((8,)),
                pltpu.SemaphoreType.DMA,
                pltpu.SemaphoreType.DMA,
                pltpu.SemaphoreType.DMA((8,)),
                pltpu.SemaphoreType.DMA((8,)),
                pltpu.SemaphoreType.DMA((CHUNKS,)),
                pltpu.SemaphoreType.DMA((CHUNKS,)),
                pltpu.SemaphoreType.DMA,
                pltpu.SemaphoreType.DMA,
                pltpu.SemaphoreType.DMA((CHUNKS,)),
                pltpu.SemaphoreType.DMA((CHUNKS,)),
            ],
            compiler_params=pltpu.CompilerParams(
                collective_id=0, has_side_effects=True, vmem_limit_bytes=40 << 20
            ),
        )(
            *(pltpu.with_memory_space_constraint(x, pltpu.HBM) for x in (
                new_source.reshape(16, 128), cap.reshape(1, SH), tr.reshape(1, SH), cell_block,
                pressure, storage, trans, source, shells_old[0],
            ))
        )
        return p, new[None]

    f = P("slab", "col")
    return jax.shard_map(
        shards,
        mesh=mesh,
        in_specs=(f, f, f, f, P("col", "slab", None, None), P(), P(), P("col", None), P("col", "slab")),
        out_specs=(f, P("col", "slab", None, None)),
        check_vma=False,
    )
```

```python
import functools

import jax
import jax.numpy as jnp
from jax import lax
from jax.experimental import pallas as pl
from jax.experimental.pallas import tpu as pltpu
from jax.sharding import PartitionSpec as P

MESH = pl.DeviceIdType.MESH
HI = lax.Precision.HIGHEST
F32, I32 = jnp.float32, jnp.int32
SLABS = 64
CHIPS = 32
SH = 64
NEW = 32
OLD = 64
STEPS, ITERS = 2, 3
IDX2, IDX3 = 16, 24


def iota(shape, dim):
    return lax.broadcasted_iota(I32, shape, dim)


def strict_upper(n):
    return (iota((n, n), 0) < iota((n, n), 1)).astype(F32)


def lane_of(d):
    return (d & 3) * 16 + (d >> 2)


def by_owner(lines):
    turned = jnp.transpose(jnp.concatenate([lines.astype(F32)] * 8, axis=0)).astype(I32)
    part = iota((NEW, 128), 1) >> 4
    tab = jnp.full((NEW, 128), -1, I32)
    for a in range(4):
        tab = jnp.where(part == a, turned[NEW * a : NEW * a + NEW, :], tab)
    return tab


def route(own, tab, out_ref):
    chip, local = tab >> 7, tab & 63
    n_of, lane32 = iota((NEW, 128), 0), iota((NEW, 128), 1)
    rank = jnp.zeros((NEW, 128), I32)
    for k in range(1, NEW):
        rank = rank + ((pltpu.roll(chip, k, 0) == chip) & (n_of >= k)).astype(I32)
    s_of = n_of
    feeds = jnp.zeros((CHIPS, 128), jnp.bool_)
    for n in range(NEW):
        feeds = feeds | (s_of == chip[n : n + 1, :])
    feeds_f = feeds.astype(F32)
    upper = strict_upper(128)
    group = jnp.dot((iota((CHIPS, CHIPS), 0) > iota((CHIPS, CHIPS), 1)).astype(F32), feeds_f).astype(I32)
    turn = jnp.dot(feeds_f, upper).astype(I32)
    place = ((turn & 7) << 7) + ((turn >> 3) << 5) + s_of
    both = jnp.where(feeds, (place << 6) + s_of, 0)
    rows = [jnp.sum(jnp.where(group == g, both, 0), axis=0, keepdims=True) for g in range(8)]
    both = jnp.concatenate(rows, axis=0)
    to_s, src = both >> 6, both & 63
    packed = jnp.where(feeds, turn * 8 + group + 1, 0).astype(F32)
    turned = jnp.transpose(jnp.concatenate([packed] * 4, axis=0)).astype(I32) - 1
    d_of, l_of = iota((128, 128), 0), iota((128, 128), 1)
    want = jnp.where(turned >= 0, (turned >> 3) - 8 * (l_of >> 5), -1)
    code = ((turned & 7) << 7) + d_of
    rows = [jnp.sum(jnp.where(want == q, code, 0), axis=0, keepdims=True) for q in range(8)]
    to_d = jnp.concatenate(rows, axis=0)

    row8, lane8 = iota((8, 128), 0), iota((8, 128), 1)
    here = (row8 << 7) + lane8

    def look(table, at):
        row, lane = at >> 7, at & 127
        out = jnp.zeros((8, 128), I32)
        for r in range(8):
            line = jnp.broadcast_to(table[r : r + 1, :], (8, 128))
            out = jnp.where(row == r, jnp.take_along_axis(line, lane, axis=1), out)
        return out

    def flip(x, k):
        for bit in (1, 2, 4):
            if k & bit:
                x = jnp.where((row8 & bit) == 0, pltpu.roll(x, 8 - bit, 0), pltpu.roll(x, bit, 0))
        return x

    def mate(x, colour, level):
        out = flip(x, level)
        for k in range(level + 1, 2 * level):
            out = jnp.where(flip(colour, k) == colour, flip(x, k), out)
        return out

    colour = jnp.zeros((8, 128), I32)
    for level, doublings in ((1, 8), (2, 7), (4, 6)):
        colour_s = look(colour, to_d) if level > 1 else colour
        partner = mate(here, colour_s, level)
        back = look(to_d, look(partner, to_s) if level > 1 else to_s ^ 128)
        hop = mate(back, colour, level)
        label = here
        for _ in range(doublings):
            got = look((hop << 10) + label, hop)
            label = jnp.minimum(label, got & 1023)
            hop = got >> 10
        colour = colour * 2 + (label > mate(label, colour, level)).astype(I32)

    colour_sd = jnp.zeros((CHIPS, 128), I32)
    colour_nd = jnp.zeros((NEW, 128), I32)
    for g in range(8):
        line, of = colour[g : g + 1, :], src[g : g + 1, :]
        colour_sd = colour_sd + jnp.where(s_of == of, line, 0)
        colour_nd = colour_nd + jnp.where(chip == of, line, 0)
    colour_sd = jnp.where(feeds, colour_sd, -1)
    masks = jnp.concatenate([(colour_sd == c).astype(F32) for c in range(8)], axis=0)
    counts = jnp.dot(masks, upper) * masks
    half = counts[0:CHIPS]
    for c in range(1, 8):
        half = half + counts[c * CHIPS : (c + 1) * CHIPS]
    half = half.astype(I32)
    own_chip = own >> 1
    mine = chip == own_chip
    slots = [
        jnp.sum(jnp.where(mine & (rank == r), local, 0), axis=0, keepdims=True) for r in range(4)
    ]
    slots = jnp.concatenate(slots + [jnp.zeros((4, 128), I32)], axis=0).astype(F32)
    own_row = s_of == own_chip
    colour_s = jnp.sum(jnp.where(own_row, colour_sd, 0), axis=0, keepdims=True)
    half_s = jnp.sum(jnp.where(own_row, half, 0), axis=0, keepdims=True)
    for h in range(2):
        pick = ((row8 == colour_s) & (half_s == h)).astype(F32)
        got = lax.dot_general(pick, slots, (((1,), (1,)), ((), ())), preferred_element_type=F32)
        out_ref[8 * h : 8 * h + 8, 0:8] = got.astype(I32) & (OLD - 1)
    take = jnp.sum(jnp.where(colour_sd == own_chip >> 2, 2 * s_of + half, 0), axis=0, keepdims=True)
    out_ref[IDX2 : IDX2 + 8, :] = jnp.broadcast_to(take & (2 * CHIPS - 1), (8, 128))
    via = colour_nd * 4 + rank
    via = jnp.sum(jnp.where(lane32 == lane_of(own), via, 0), axis=1, keepdims=True)
    out_ref[IDX3 : IDX3 + NEW, :] = jnp.broadcast_to(via & (CHIPS - 1), (NEW, 128))


def matrices(cap_in, trans_in, out_ref):
    shape = (SH, 128)
    k_of, lane = iota(shape, 0), iota(shape, 1)
    eye = k_of == lane

    def column(row):
        square = iota((SH, SH), 0) == iota((SH, SH), 1)
        return jnp.broadcast_to(jnp.sum(jnp.where(square, row, 0.0), axis=1, keepdims=True), shape)

    cap, tr = column(cap_in), column(trans_in)
    cap_row = jnp.sum(jnp.where(eye, cap, 0.0), axis=0, keepdims=True)
    inner = jnp.where(k_of == SH - 1, 0.0, pltpu.roll(tr, SH - 1, 0))
    t0 = jnp.broadcast_to(tr[0:1, :], shape)
    b = cap + tr + inner
    c = -inner
    a = jnp.where(k_of == 0, 0.0, -tr)
    rhs = eye.astype(F32)
    s = 1
    while s < SH:
        up, down = (lambda x: pltpu.roll(x, s, 0)), (lambda x: pltpu.roll(x, SH - s, 0))
        al, ga = -a / up(b), -c / down(b)
        rhs = rhs + al * up(rhs) + ga * down(rhs)
        b = b + al * up(c) + ga * down(a)
        a, c = al * up(a), ga * down(c)
        s *= 2
    inverse = rhs / b
    amat = inverse * cap_row
    couple = jnp.broadcast_to(inverse[:, 0:1], shape) * t0
    asq = jnp.dot(amat[:, :SH], amat, precision=HI, preferred_element_type=F32)
    acouple = jnp.dot(amat[:, :SH], couple, precision=HI, preferred_element_type=F32)
    out_ref[0] = asq
    out_ref[1] = t0 * column(amat[0:1, :SH])
    out_ref[2] = t0 * column(asq[0:1, :SH])
    out_ref[3] = acouple
    out_ref[4] = couple
    out_ref[5, 0:8, :] = t0[0:8] * (1.0 - jnp.broadcast_to(couple[0:1], (8, 128)))
    out_ref[5, 8:16, :] = t0[0:8] * jnp.broadcast_to(acouple[0:1], (8, 128))


WIDE = 8
PARTS = (40, 24)
CHUNKS = len(PARTS)
DEFAULTS = (1.0, 1.0, 0.0, 0.0, 0.0, 0.0, 0.0)
NF = len(DEFAULTS)
HALO = 2 * WIDE


def move_kernel(
    slabs, cols,
    table_hbm, cap_hbm, trans_row_hbm, cb_hbm, p_hbm, storage_hbm, trans_hbm, source_hbm, old_hbm,
    p_out, new_out,
    table_ref, cap_ref, trans_row_ref, cb_ref, old_ref, mat_ref, tbl_ref, tbl,
    field, rows_in, edge_l, edge_r, from_l, from_r, line1, line2, shells1, shells2,
    stage1, mid, stage2, got, pb_stage, pb_mid,
    load, load_old, load_tbl, halo_send, halo_recv, send1, recv1, send_pb, recv_pb, send2, recv2,
):
    own, col = lax.axis_index("slab"), lax.axis_index("col")
    chip = own // 2
    first_core, second_core = own % 2 == 0, own % 2 == 1
    loads = [
        pltpu.make_async_copy(src, dst, load.at[i])
        for i, (src, dst) in enumerate((
            (table_hbm, table_ref), (cap_hbm, cap_ref), (trans_row_hbm, trans_row_ref), (cb_hbm, cb_ref),
            (p_hbm, field.at[0]), (storage_hbm, field.at[1]), (trans_hbm, field.at[2]), (source_hbm, field.at[3]),
        ))
    ]
    old_load = pltpu.make_async_copy(old_hbm, old_ref, load_old)
    for one in loads:
        one.start()

    @pl.when(first_core)
    def _():
        old_load.start()

    neighbours = []
    for dr, dc in ((-1, 0), (1, 0), (0, -1), (0, 1), (-1, -1), (1, -1), (-1, 1), (1, 1)):
        ok = None
        for step, at, size in ((dr, own, slabs), (dc, col, cols)):
            if step:
                inside = at > 0 if step < 0 else at < size - 1
                ok = inside if ok is None else ok & inside
        neighbours.append((ok, dr, dc))

    lane80 = iota((80, 128), 1)
    for f, value in enumerate(DEFAULTS):
        rows_in[f] = jnp.full((HALO, 256), value, F32)
    default = jnp.full((80, 128), 0.0, F32)
    for f, value in enumerate(DEFAULTS):
        if value:
            default = jnp.where(lane80 // WIDE == f, value, default)
    from_l[...] = default
    from_r[...] = default

    barrier = pltpu.get_barrier_semaphore()

    def greet(slab, c):
        pl.semaphore_signal(barrier, inc=1, device_id={"slab": slab, "col": c}, device_id_type=MESH)

    for ok, dr, dc in neighbours:
        if dc:
            @pl.when(ok)
            def _():
                greet(own + dr, col + dc)

    @pl.when(first_core)
    def _():
        def body(k, _):
            greet(2 * ((chip + k) % CHIPS) + 1, col)
            return 0
        lax.fori_loop(0, CHIPS, body, 0)

    @pl.when(second_core)
    def _():
        def body(k, _):
            greet((own + k) % slabs, col)
            return 0
        lax.fori_loop(1, slabs, body, 0)

    for one in loads:
        one.wait()
    matrices(cap_ref[...], trans_row_ref[...], mat_ref)
    route(own, by_owner(table_ref[...]), tbl_ref)
    tbl_copy = pltpu.make_async_copy(tbl_ref, tbl, load_tbl)
    tbl_copy.start()

    weight1, weight2 = mat_ref[1], mat_ref[2]

    @pl.when(first_core)
    def _():
        old_load.wait()

        def body(o, _):
            first, second = [], []
            for j in range(8):
                x = old_ref[8 * o + j]
                first.append(jnp.sum(x * weight1, axis=0, keepdims=True))
                second.append(jnp.sum(x * weight2, axis=0, keepdims=True))
            shells1[pl.ds(8 * o, 8), :] = jnp.concatenate(first, axis=0)
            shells2[pl.ds(8 * o, 8), :] = jnp.concatenate(second, axis=0)
            return 0
        lax.fori_loop(0, OLD // 8, body, 0)

    row64 = iota((64, 64), 0)
    blocks = cb_ref[...]
    hot = [(blocks == 2 * row64 + h).astype(F32) for h in range(2)]

    @pl.when(first_core)
    def _():
        for h in range(2):
            part = pl.ds(128 * h, 128)
            field[4, :, part] = jnp.dot(hot[h], shells1[...], precision=HI, preferred_element_type=F32)
            field[5, :, part] = jnp.dot(hot[h], shells2[...], precision=HI, preferred_element_type=F32)
            field[6, :, part] = jnp.broadcast_to(jnp.sum(hot[h], axis=1, keepdims=True), (64, 128))

    @pl.when(second_core)
    def _():
        for f in range(4, 7):
            field[f] = jnp.zeros((64, 256), F32)

    lane64 = iota((64, 128), 1)
    left, right = jnp.zeros((64, 128), F32), jnp.zeros((64, 128), F32)
    for f in range(NF):
        spot = lane64 // WIDE == f
        a, b = field[f, :, 0:128], field[f, :, 128:256]
        left = jnp.where(spot, pltpu.roll(a, WIDE * f, 1) if f else a, left)
        right = jnp.where(spot, pltpu.roll(b, WIDE * (f + 1), 1), right)
    edge_l[...] = left
    edge_r[...] = right

    extra = (col > 0).astype(I32) + (col < cols - 1).astype(I32)
    near = 1 + (own > 0).astype(I32) + (own < slabs - 1).astype(I32)
    pl.semaphore_wait(barrier, extra * near + jnp.where(first_core, CHIPS, slabs - 1))

    def copy_of(i, dr, dc):
        if dc == 0:
            src = field.at[:, pl.ds(0 if dr < 0 else 64 - WIDE, WIDE), :]
            dst = rows_in.at[:, pl.ds(WIDE if dr > 0 else 0, WIDE), :]
        else:
            src, dst = (edge_l, from_r) if dc < 0 else (edge_r, from_l)
            if dr == 0:
                dst = dst.at[pl.ds(0, 64), :]
            else:
                src = src.at[pl.ds(0 if dr < 0 else 64 - WIDE, WIDE), :]
                dst = dst.at[pl.ds(64 + (WIDE if dr > 0 else 0), WIDE), :]
        return pltpu.make_async_remote_copy(
            src_ref=src, dst_ref=dst, send_sem=halo_send.at[i], recv_sem=halo_recv.at[i],
            device_id={"slab": own + dr, "col": col + dc}, device_id_type=MESH,
        )

    for i, (ok, dr, dc) in enumerate(neighbours):
        @pl.when(ok)
        def _():
            copy_of(i, dr, dc).start()

    def to_middle(src, dst, send, recv, m):
        return pltpu.make_async_remote_copy(
            src_ref=src, dst_ref=dst, send_sem=send, recv_sem=recv,
            device_id={"slab": 2 * m + 1}, device_id_type=MESH,
        )

    def rows_of(c):
        return pl.ds(sum(PARTS[:c]), PARTS[c])

    def chunk_to_middle(c, m):
        src, dst = stage1.at[pl.ds(2 * m, 2), rows_of(c)], mid[c].at[pl.ds(2 * chip, 2)]
        to_middle(src, dst, send1.at[c], recv1.at[c], m).start()

    tbl_copy.wait()

    @pl.when(first_core)
    def _():
        square = mat_ref[0][:, :SH]

        def body(k, _):
            m = (chip + k) % CHIPS
            for h in range(2):
                slot = tbl[8 * h + m // 4, m % 4]
                stage1[2 * m + h] = jnp.dot(square, old_ref[slot], precision=HI, preferred_element_type=F32)
            chunk_to_middle(0, m)
            return 0
        lax.fori_loop(0, CHIPS, body, 0)

    for i, (ok, dr, dc) in enumerate(neighbours):
        back = next(b for b, n in enumerate(neighbours) if n[1:] == (-dr, -dc))
        @pl.when(neighbours[back][0])
        def _():
            copy_of(i, dr, dc).wait_recv()

    shape = (64 + HALO, 384)
    in_l, in_r = from_l[...], from_r[...]

    def extended(f):
        rows = jnp.concatenate([field[f], rows_in[f]], axis=0)
        tail = jnp.where(lane80 >= 128 - WIDE, pltpu.roll(in_l, (128 - WIDE * (f + 1)) % 128, 1), DEFAULTS[f])
        tail = jnp.where(lane80 < WIDE, pltpu.roll(in_r, (128 - WIDE * f) % 128, 1), tail)
        return jnp.concatenate([rows, tail], axis=1)

    def after(x, axis):
        return pltpu.roll(x, shape[axis] - 1, axis)

    def before(x, axis):
        return pltpu.roll(x, 1, axis)

    p, storage, trans, source, base1, base2, active = [extended(f) for f in range(NF)]
    kappa, cross = mat_ref[5, 0:1, 0:1], mat_ref[5, 8:9, 0:1]
    faces = []
    for axis in (1, 0):
        other = after(trans, axis)
        total = trans + other
        faces.append(2.0 * trans * other / jnp.where(total == 0.0, 1.0, total))
    conduct = faces[0] + before(faces[0], 1) + faces[1] + before(faces[1], 0)
    draw = active * kappa
    slope0 = storage + draw
    half = [0.5 * x for x in faces]
    base = base1
    for step, line in ((0, line1), (1, line2)):
        prev = p
        for sweep in range(ITERS):
            if sweep == ITERS - 1:
                line[...] = p[0:64, 0:256]
                if step == 0:
                    base = base2 + active * (cross * p)
            flux = jnp.zeros(shape, F32)
            for axis, face in zip((1, 0), half):
                other = after(p, axis)
                flow = face * (other + p) * (other - p)
                flux = flux + flow - before(flow, axis)
            misfit = storage * (p - prev) - flux + (draw * p - (base1 if step == 0 else base)) - source
            p = p - misfit / (slope0 + p * conduct)
    p_out[...] = p[0:64, 0:256]

    @pl.when(first_core)
    def _():
        for line, rows in ((line1, shells1), (line2, shells2)):
            total = jnp.zeros((OLD, 128), F32)
            for h in range(2):
                total = total + lax.dot_general(
                    hot[h], line[:, 128 * h : 128 * h + 128], (((0,), (0,)), ((), ())),
                    precision=HI, preferred_element_type=F32,
                )
            rows[...] = total

        def body(k, _):
            m = (chip + k) % CHIPS
            for h in range(2):
                slot = tbl[8 * h + m // 4, m % 4]
                pb_stage[m, pl.ds(h, 1), :] = shells1[pl.ds(slot, 1), :]
                pb_stage[m, pl.ds(2 + h, 1), :] = shells2[pl.ds(slot, 1), :]
            for r in range(4, 8):
                pb_stage[m, pl.ds(r, 1), :] = jnp.zeros((1, 128), F32)
            to_middle(pb_stage.at[m], pb_mid.at[chip], send_pb, recv_pb, m).start()
            return 0
        lax.fori_loop(0, CHIPS, body, 0)

        for c in range(1, CHUNKS):
            def later(k, _):
                chunk_to_middle(c, (chip + k) % CHIPS)
                return 0
            lax.fori_loop(0, CHIPS, later, 0)

    def await_bytes(ref, sem):
        pltpu.make_async_copy(ref, ref, sem).wait()

    @pl.when(second_core)
    def _():
        for c in range(CHUNKS):
            rows = rows_of(c)
            await_bytes(mid[c], recv1.at[c])
            if c == 0:
                await_bytes(pb_mid, recv_pb)
            acouple, couple = mat_ref[3, rows], mat_ref[4, rows]

            def block(d):
                i = tbl[IDX2, lane_of(d)]
                s, h = i // 2, i % 2
                first = pb_mid[s, pl.ds(h, 1), :]
                second = pb_mid[s, pl.ds(2 + h, 1), :]
                return mid[c][i] + acouple * first + couple * second

            def body(k, _):
                d = (own + k) % slabs
                stage2[d, rows] = block(d)
                pltpu.make_async_remote_copy(
                    src_ref=stage2.at[d, rows], dst_ref=got[c].at[chip], send_sem=send2.at[c], recv_sem=recv2.at[c],
                    device_id={"slab": d}, device_id_type=MESH,
                ).start()
                return 0
            lax.fori_loop(1, slabs, body, 0)
            got[c][chip] = block(own)

    for c in range(CHUNKS):
        @pl.when(second_core)
        def _():
            await_bytes(got[c].at[pl.ds(0, CHIPS - 1)], recv2.at[c])

        @pl.when(first_core)
        def _():
            await_bytes(got[c], recv2.at[c])

        def gather(n, _):
            for j in range(4):
                new_out[4 * n + j, rows_of(c)] = got[c][tbl[IDX3 + 4 * n + j, 0]]
            return 0
        lax.fori_loop(0, NEW // 4, gather, 0)

    for i, (ok, dr, dc) in enumerate(neighbours):
        @pl.when(ok)
        def _():
            copy_of(i, dr, dc).wait_send()

    @pl.when(first_core)
    def _():
        for c in range(CHUNKS):
            await_bytes(stage1.at[:, rows_of(c)], send1.at[c])
        await_bytes(pb_stage, send_pb)

    @pl.when(second_core)
    def _():
        for c in range(CHUNKS):
            await_bytes(stage2.at[pl.ds(0, 2 * CHIPS - 1), rows_of(c)], send2.at[c])


def solution(mesh):
    slabs, cols = mesh.shape["slab"], mesh.shape["col"]

    def shards(pressure, storage, trans, source, shells_old, cap, tr, new_source, cell_block):
        vmem = pl.BlockSpec(memory_space=pltpu.VMEM)
        p, new = pl.pallas_call(
            functools.partial(move_kernel, slabs, cols),
            out_shape=(
                jax.ShapeDtypeStruct((64, 256), F32),
                jax.ShapeDtypeStruct((NEW, SH, 128), F32),
            ),
            in_specs=[pl.BlockSpec(memory_space=pl.ANY)] * 9,
            out_specs=[vmem] * 2,
            scratch_shapes=[
                pltpu.VMEM((16, 128), I32),
                pltpu.VMEM((1, SH), F32),
                pltpu.VMEM((1, SH), F32),
                pltpu.VMEM((1, OLD), I32),
                pltpu.VMEM((OLD, SH, 128), F32),
                pltpu.VMEM((6, SH, 128), F32),
                pltpu.VMEM((56, 128), I32),
                pltpu.SMEM((56, 128), I32),
                pltpu.VMEM((NF, 64, 256), F32),
                pltpu.VMEM((NF, HALO, 256), F32),
                pltpu.VMEM((64, 128), F32),
                pltpu.VMEM((64, 128), F32),
                pltpu.VMEM((80, 128), F32),
                pltpu.VMEM((80, 128), F32),
                pltpu.VMEM((64, 256), F32),
                pltpu.VMEM((64, 256), F32),
                pltpu.VMEM((OLD, 128), F32),
                pltpu.VMEM((OLD, 128), F32),
                pltpu.VMEM((2 * CHIPS, SH, 128), F32),
                tuple(pltpu.VMEM((2 * CHIPS, part, 128), F32) for part in PARTS),
                pltpu.VMEM((2 * CHIPS, SH, 128), F32),
                tuple(pltpu.VMEM((CHIPS, part, 128), F32) for part in PARTS),
                pltpu.VMEM((CHIPS, 8, 128), F32),
                pltpu.VMEM((CHIPS, 8, 128), F32),
                pltpu.SemaphoreType.DMA((8,)),
                pltpu.SemaphoreType.DMA,
                pltpu.SemaphoreType.DMA,
                pltpu.SemaphoreType.DMA((8,)),
                pltpu.SemaphoreType.DMA((8,)),
                pltpu.SemaphoreType.DMA((CHUNKS,)),
                pltpu.SemaphoreType.DMA((CHUNKS,)),
                pltpu.SemaphoreType.DMA,
                pltpu.SemaphoreType.DMA,
                pltpu.SemaphoreType.DMA((CHUNKS,)),
                pltpu.SemaphoreType.DMA((CHUNKS,)),
            ],
            compiler_params=pltpu.CompilerParams(
                collective_id=0, has_side_effects=True, vmem_limit_bytes=40 << 20
            ),
        )(
            *(pltpu.with_memory_space_constraint(x, pltpu.HBM) for x in (
                new_source.reshape(16, 128), cap.reshape(1, SH), tr.reshape(1, SH), cell_block,
                pressure, storage, trans, source, shells_old[0],
            ))
        )
        return p, new[None]

    f = P("slab", "col")
    return jax.shard_map(
        shards,
        mesh=mesh,
        in_specs=(f, f, f, f, P("col", "slab", None, None), P(), P(), P("col", None), P("col", "slab")),
        out_specs=(f, P("col", "slab", None, None)),
        check_vma=False,
    )
```

```python
import functools

import jax
import jax.numpy as jnp
from jax import lax
from jax.experimental import pallas as pl
from jax.experimental.pallas import tpu as pltpu
from jax.sharding import PartitionSpec as P

MESH = pl.DeviceIdType.MESH
HI = lax.Precision.HIGHEST
F32, I32 = jnp.float32, jnp.int32
SLABS = 64
CHIPS = 32
SH = 64
NEW = 32
OLD = 64
STEPS, ITERS = 2, 3
IDX2, IDX3 = 16, 24


def iota(shape, dim):
    return lax.broadcasted_iota(I32, shape, dim)


def strict_upper(n):
    return (iota((n, n), 0) < iota((n, n), 1)).astype(F32)


def lane_of(d):
    return (d & 3) * 16 + (d >> 2)


def by_owner(lines):
    turned = jnp.transpose(jnp.concatenate([lines.astype(F32)] * 8, axis=0)).astype(I32)
    part = iota((NEW, 128), 1) >> 4
    tab = jnp.full((NEW, 128), -1, I32)
    for a in range(4):
        tab = jnp.where(part == a, turned[NEW * a : NEW * a + NEW, :], tab)
    return tab


def route(own, tab, out_ref):
    chip, local = tab >> 7, tab & 63
    n_of, lane32 = iota((NEW, 128), 0), iota((NEW, 128), 1)
    rank = jnp.zeros((NEW, 128), I32)
    for k in range(1, NEW):
        rank = rank + ((pltpu.roll(chip, k, 0) == chip) & (n_of >= k)).astype(I32)
    s_of = n_of
    feeds = jnp.zeros((CHIPS, 128), jnp.bool_)
    for n in range(NEW):
        feeds = feeds | (s_of == chip[n : n + 1, :])
    feeds_f = feeds.astype(F32)
    upper = strict_upper(128)
    group = jnp.dot((iota((CHIPS, CHIPS), 0) > iota((CHIPS, CHIPS), 1)).astype(F32), feeds_f).astype(I32)
    turn = jnp.dot(feeds_f, upper).astype(I32)
    place = ((turn & 7) << 7) + ((turn >> 3) << 5) + s_of
    both = jnp.where(feeds, (place << 6) + s_of, 0)
    rows = [jnp.sum(jnp.where(group == g, both, 0), axis=0, keepdims=True) for g in range(8)]
    both = jnp.concatenate(rows, axis=0)
    to_s, src = both >> 6, both & 63
    packed = jnp.where(feeds, turn * 8 + group + 1, 0).astype(F32)
    turned = jnp.transpose(jnp.concatenate([packed] * 4, axis=0)).astype(I32) - 1
    d_of, l_of = iota((128, 128), 0), iota((128, 128), 1)
    want = jnp.where(turned >= 0, (turned >> 3) - 8 * (l_of >> 5), -1)
    code = ((turned & 7) << 7) + d_of
    rows = [jnp.sum(jnp.where(want == q, code, 0), axis=0, keepdims=True) for q in range(8)]
    to_d = jnp.concatenate(rows, axis=0)

    row8, lane8 = iota((8, 128), 0), iota((8, 128), 1)
    here = (row8 << 7) + lane8

    def look(table, at):
        row, lane = at >> 7, at & 127
        out = jnp.zeros((8, 128), I32)
        for r in range(8):
            line = jnp.broadcast_to(table[r : r + 1, :], (8, 128))
            out = jnp.where(row == r, jnp.take_along_axis(line, lane, axis=1), out)
        return out

    def flip(x, k):
        for bit in (1, 2, 4):
            if k & bit:
                x = jnp.where((row8 & bit) == 0, pltpu.roll(x, 8 - bit, 0), pltpu.roll(x, bit, 0))
        return x

    def mate(x, colour, level):
        out = flip(x, level)
        for k in range(level + 1, 2 * level):
            out = jnp.where(flip(colour, k) == colour, flip(x, k), out)
        return out

    colour = jnp.zeros((8, 128), I32)
    for level, doublings in ((1, 8), (2, 7), (4, 6)):
        colour_s = look(colour, to_d) if level > 1 else colour
        partner = mate(here, colour_s, level)
        back = look(to_d, look(partner, to_s) if level > 1 else to_s ^ 128)
        hop = mate(back, colour, level)
        label = here
        for _ in range(doublings):
            got = look((hop << 10) + label, hop)
            label = jnp.minimum(label, got & 1023)
            hop = got >> 10
        colour = colour * 2 + (label > mate(label, colour, level)).astype(I32)

    colour_sd = jnp.zeros((CHIPS, 128), I32)
    colour_nd = jnp.zeros((NEW, 128), I32)
    for g in range(8):
        line, of = colour[g : g + 1, :], src[g : g + 1, :]
        colour_sd = colour_sd + jnp.where(s_of == of, line, 0)
        colour_nd = colour_nd + jnp.where(chip == of, line, 0)
    colour_sd = jnp.where(feeds, colour_sd, -1)
    masks = jnp.concatenate([(colour_sd == c).astype(F32) for c in range(8)], axis=0)
    counts = jnp.dot(masks, upper) * masks
    half = counts[0:CHIPS]
    for c in range(1, 8):
        half = half + counts[c * CHIPS : (c + 1) * CHIPS]
    half = half.astype(I32)
    own_chip = own >> 1
    mine = chip == own_chip
    slots = [
        jnp.sum(jnp.where(mine & (rank == r), local, 0), axis=0, keepdims=True) for r in range(4)
    ]
    slots = jnp.concatenate(slots + [jnp.zeros((4, 128), I32)], axis=0).astype(F32)
    own_row = s_of == own_chip
    colour_s = jnp.sum(jnp.where(own_row, colour_sd, 0), axis=0, keepdims=True)
    half_s = jnp.sum(jnp.where(own_row, half, 0), axis=0, keepdims=True)
    for h in range(2):
        pick = ((row8 == colour_s) & (half_s == h)).astype(F32)
        got = lax.dot_general(pick, slots, (((1,), (1,)), ((), ())), preferred_element_type=F32)
        out_ref[8 * h : 8 * h + 8, 0:8] = got.astype(I32) & (OLD - 1)
    take = jnp.sum(jnp.where(colour_sd == own_chip >> 2, 2 * s_of + half, 0), axis=0, keepdims=True)
    out_ref[IDX2 : IDX2 + 8, :] = jnp.broadcast_to(take & (2 * CHIPS - 1), (8, 128))
    via = colour_nd * 4 + rank
    via = jnp.sum(jnp.where(lane32 == lane_of(own), via, 0), axis=1, keepdims=True)
    out_ref[IDX3 : IDX3 + NEW, :] = jnp.broadcast_to(via & (CHIPS - 1), (NEW, 128))


def matrices(cap_in, trans_in, out_ref):
    shape = (SH, 128)
    k_of, lane = iota(shape, 0), iota(shape, 1)
    eye = k_of == lane

    def column(row):
        square = iota((SH, SH), 0) == iota((SH, SH), 1)
        return jnp.broadcast_to(jnp.sum(jnp.where(square, row, 0.0), axis=1, keepdims=True), shape)

    cap, tr = column(cap_in), column(trans_in)
    cap_row = jnp.sum(jnp.where(eye, cap, 0.0), axis=0, keepdims=True)
    inner = jnp.where(k_of == SH - 1, 0.0, pltpu.roll(tr, SH - 1, 0))
    t0 = jnp.broadcast_to(tr[0:1, :], shape)
    b = cap + tr + inner
    c = -inner
    a = jnp.where(k_of == 0, 0.0, -tr)
    rhs = eye.astype(F32)
    s = 1
    while s < SH:
        up, down = (lambda x: pltpu.roll(x, s, 0)), (lambda x: pltpu.roll(x, SH - s, 0))
        al, ga = -a / up(b), -c / down(b)
        rhs = rhs + al * up(rhs) + ga * down(rhs)
        b = b + al * up(c) + ga * down(a)
        a, c = al * up(a), ga * down(c)
        s *= 2
    inverse = rhs / b
    amat = inverse * cap_row
    couple = jnp.broadcast_to(inverse[:, 0:1], shape) * t0
    asq = jnp.dot(amat[:, :SH], amat, precision=HI, preferred_element_type=F32)
    acouple = jnp.dot(amat[:, :SH], couple, precision=HI, preferred_element_type=F32)
    out_ref[0] = asq
    out_ref[1] = t0 * column(amat[0:1, :SH])
    out_ref[2] = t0 * column(asq[0:1, :SH])
    out_ref[3] = acouple
    out_ref[4] = couple
    out_ref[5, 0:8, :] = t0[0:8] * (1.0 - jnp.broadcast_to(couple[0:1], (8, 128)))
    out_ref[5, 8:16, :] = t0[0:8] * jnp.broadcast_to(acouple[0:1], (8, 128))


WIDE = 8
PARTS = (40, 24)
CHUNKS = len(PARTS)
DEFAULTS = (1.0, 1.0, 0.0, 0.0, 0.0, 0.0, 0.0)
NF = len(DEFAULTS)
HALO = 2 * WIDE


def move_kernel(
    slabs, cols,
    table_hbm, cap_hbm, trans_row_hbm, cb_hbm, p_hbm, storage_hbm, trans_hbm, source_hbm, old_hbm,
    p_out, new_out,
    table_ref, cap_ref, trans_row_ref, cb_ref, old_ref, mat_ref, tbl_ref, tbl,
    field, rows_in, edge_l, edge_r, from_l, from_r, line1, line2, shells1, shells2,
    stage1, mid, stage2, got, pb_stage, pb_mid,
    load, load_old, load_tbl, halo_send, halo_recv, send1, recv1, send_pb, recv_pb, send2, recv2,
):
    own, col = lax.axis_index("slab"), lax.axis_index("col")
    chip = own // 2
    first_core, second_core = own % 2 == 0, own % 2 == 1
    loads = [
        pltpu.make_async_copy(src, dst, load.at[i])
        for i, (src, dst) in enumerate((
            (table_hbm, table_ref), (cap_hbm, cap_ref), (trans_row_hbm, trans_row_ref), (cb_hbm, cb_ref),
            (p_hbm, field.at[0]), (storage_hbm, field.at[1]), (trans_hbm, field.at[2]), (source_hbm, field.at[3]),
        ))
    ]
    old_load = pltpu.make_async_copy(old_hbm, old_ref, load_old)
    for one in loads:
        one.start()

    @pl.when(first_core)
    def _():
        old_load.start()

    neighbours = []
    for dr, dc in ((-1, 0), (1, 0), (0, -1), (0, 1), (-1, -1), (1, -1), (-1, 1), (1, 1)):
        ok = None
        for step, at, size in ((dr, own, slabs), (dc, col, cols)):
            if step:
                inside = at > 0 if step < 0 else at < size - 1
                ok = inside if ok is None else ok & inside
        neighbours.append((ok, dr, dc))

    lane80 = iota((80, 128), 1)
    for f, value in enumerate(DEFAULTS):
        rows_in[f] = jnp.full((HALO, 256), value, F32)
    default = jnp.full((80, 128), 0.0, F32)
    for f, value in enumerate(DEFAULTS):
        if value:
            default = jnp.where(lane80 // WIDE == f, value, default)
    from_l[...] = default
    from_r[...] = default

    barrier = pltpu.get_barrier_semaphore()

    def greet(slab, c):
        pl.semaphore_signal(barrier, inc=1, device_id={"slab": slab, "col": c}, device_id_type=MESH)

    for ok, dr, dc in neighbours:
        if dc:
            @pl.when(ok)
            def _():
                greet(own + dr, col + dc)

    @pl.when(first_core)
    def _():
        def body(k, _):
            for j in range(8):
                greet(2 * ((chip + 8 * k + j) % CHIPS) + 1, col)
            return 0
        lax.fori_loop(0, CHIPS // 8, body, 0)

    @pl.when(second_core)
    def _():
        def body(k, _):
            for j in range(9):
                greet((own + 9 * k + j + 1) % slabs, col)
            return 0
        lax.fori_loop(0, (slabs - 1) // 9, body, 0)

    for one in loads:
        one.wait()
    matrices(cap_ref[...], trans_row_ref[...], mat_ref)
    route(own, by_owner(table_ref[...]), tbl_ref)
    tbl_copy = pltpu.make_async_copy(tbl_ref, tbl, load_tbl)
    tbl_copy.start()

    weight1, weight2 = mat_ref[1], mat_ref[2]

    @pl.when(first_core)
    def _():
        old_load.wait()

        def body(o, _):
            first, second = [], []
            for j in range(8):
                x = old_ref[8 * o + j]
                first.append(jnp.sum(x * weight1, axis=0, keepdims=True))
                second.append(jnp.sum(x * weight2, axis=0, keepdims=True))
            shells1[pl.ds(8 * o, 8), :] = jnp.concatenate(first, axis=0)
            shells2[pl.ds(8 * o, 8), :] = jnp.concatenate(second, axis=0)
            return 0
        lax.fori_loop(0, OLD // 8, body, 0)

    row64 = iota((64, 64), 0)
    blocks = cb_ref[...]
    hot = [(blocks == 2 * row64 + h).astype(F32) for h in range(2)]

    @pl.when(first_core)
    def _():
        for h in range(2):
            part = pl.ds(128 * h, 128)
            field[4, :, part] = jnp.dot(hot[h], shells1[...], precision=HI, preferred_element_type=F32)
            field[5, :, part] = jnp.dot(hot[h], shells2[...], precision=HI, preferred_element_type=F32)
            field[6, :, part] = jnp.broadcast_to(jnp.sum(hot[h], axis=1, keepdims=True), (64, 128))

    @pl.when(second_core)
    def _():
        for f in range(4, 7):
            field[f] = jnp.zeros((64, 256), F32)

    lane64 = iota((64, 128), 1)
    left, right = jnp.zeros((64, 128), F32), jnp.zeros((64, 128), F32)
    for f in range(NF):
        spot = lane64 // WIDE == f
        a, b = field[f, :, 0:128], field[f, :, 128:256]
        left = jnp.where(spot, pltpu.roll(a, WIDE * f, 1) if f else a, left)
        right = jnp.where(spot, pltpu.roll(b, WIDE * (f + 1), 1), right)
    edge_l[...] = left
    edge_r[...] = right

    extra = (col > 0).astype(I32) + (col < cols - 1).astype(I32)
    near = 1 + (own > 0).astype(I32) + (own < slabs - 1).astype(I32)
    pl.semaphore_wait(barrier, extra * near + jnp.where(first_core, CHIPS, slabs - 1))

    def copy_of(i, dr, dc):
        if dc == 0:
            src = field.at[:, pl.ds(0 if dr < 0 else 64 - WIDE, WIDE), :]
            dst = rows_in.at[:, pl.ds(WIDE if dr > 0 else 0, WIDE), :]
        else:
            src, dst = (edge_l, from_r) if dc < 0 else (edge_r, from_l)
            if dr == 0:
                dst = dst.at[pl.ds(0, 64), :]
            else:
                src = src.at[pl.ds(0 if dr < 0 else 64 - WIDE, WIDE), :]
                dst = dst.at[pl.ds(64 + (WIDE if dr > 0 else 0), WIDE), :]
        return pltpu.make_async_remote_copy(
            src_ref=src, dst_ref=dst, send_sem=halo_send.at[i], recv_sem=halo_recv.at[i],
            device_id={"slab": own + dr, "col": col + dc}, device_id_type=MESH,
        )

    for i, (ok, dr, dc) in enumerate(neighbours):
        @pl.when(ok)
        def _():
            copy_of(i, dr, dc).start()

    def to_middle(src, dst, send, recv, m):
        return pltpu.make_async_remote_copy(
            src_ref=src, dst_ref=dst, send_sem=send, recv_sem=recv,
            device_id={"slab": 2 * m + 1}, device_id_type=MESH,
        )

    def rows_of(c):
        return pl.ds(sum(PARTS[:c]), PARTS[c])

    def chunk_to_middle(c, m):
        src, dst = stage1.at[pl.ds(2 * m, 2), rows_of(c)], mid[c].at[pl.ds(2 * chip, 2)]
        to_middle(src, dst, send1.at[c], recv1.at[c], m).start()

    tbl_copy.wait()

    @pl.when(first_core)
    def _():
        square = mat_ref[0][:, :SH]

        def body(k, _):
            m = (chip + k) % CHIPS
            for h in range(2):
                slot = tbl[8 * h + m // 4, m % 4]
                stage1[2 * m + h] = jnp.dot(square, old_ref[slot], precision=HI, preferred_element_type=F32)
            chunk_to_middle(0, m)
            return 0
        lax.fori_loop(0, CHIPS, body, 0)

    for i, (ok, dr, dc) in enumerate(neighbours):
        back = next(b for b, n in enumerate(neighbours) if n[1:] == (-dr, -dc))
        @pl.when(neighbours[back][0])
        def _():
            copy_of(i, dr, dc).wait_recv()

    shape = (64 + HALO, 384)
    in_l, in_r = from_l[...], from_r[...]

    def extended(f):
        rows = jnp.concatenate([field[f], rows_in[f]], axis=0)
        tail = jnp.where(lane80 >= 128 - WIDE, pltpu.roll(in_l, (128 - WIDE * (f + 1)) % 128, 1), DEFAULTS[f])
        tail = jnp.where(lane80 < WIDE, pltpu.roll(in_r, (128 - WIDE * f) % 128, 1), tail)
        return jnp.concatenate([rows, tail], axis=1)

    def after(x, axis):
        return pltpu.roll(x, shape[axis] - 1, axis)

    def before(x, axis):
        return pltpu.roll(x, 1, axis)

    p, storage, trans, source, base1, base2, active = [extended(f) for f in range(NF)]
    kappa, cross = mat_ref[5, 0:1, 0:1], mat_ref[5, 8:9, 0:1]
    faces = []
    for axis in (1, 0):
        other = after(trans, axis)
        total = trans + other
        faces.append(2.0 * trans * other / jnp.where(total == 0.0, 1.0, total))
    conduct = faces[0] + before(faces[0], 1) + faces[1] + before(faces[1], 0)
    draw = active * kappa
    slope0 = storage + draw
    half = [0.5 * x for x in faces]
    base = base1
    for step, line in ((0, line1), (1, line2)):
        prev = p
        for sweep in range(ITERS):
            if sweep == ITERS - 1:
                line[...] = p[0:64, 0:256]
                if step == 0:
                    base = base2 + active * (cross * p)
            flux = jnp.zeros(shape, F32)
            for axis, face in zip((1, 0), half):
                other = after(p, axis)
                flow = face * (other + p) * (other - p)
                flux = flux + flow - before(flow, axis)
            misfit = storage * (p - prev) - flux + (draw * p - (base1 if step == 0 else base)) - source
            p = p - misfit / (slope0 + p * conduct)
    p_out[...] = p[0:64, 0:256]

    @pl.when(first_core)
    def _():
        for line, rows in ((line1, shells1), (line2, shells2)):
            total = jnp.zeros((OLD, 128), F32)
            for h in range(2):
                total = total + lax.dot_general(
                    hot[h], line[:, 128 * h : 128 * h + 128], (((0,), (0,)), ((), ())),
                    precision=HI, preferred_element_type=F32,
                )
            rows[...] = total

        def body(k, _):
            m = (chip + k) % CHIPS
            for h in range(2):
                slot = tbl[8 * h + m // 4, m % 4]
                pb_stage[m, pl.ds(h, 1), :] = shells1[pl.ds(slot, 1), :]
                pb_stage[m, pl.ds(2 + h, 1), :] = shells2[pl.ds(slot, 1), :]
            for r in range(4, 8):
                pb_stage[m, pl.ds(r, 1), :] = jnp.zeros((1, 128), F32)
            to_middle(pb_stage.at[m], pb_mid.at[chip], send_pb, recv_pb, m).start()
            return 0
        lax.fori_loop(0, CHIPS, body, 0)

        for c in range(1, CHUNKS):
            def later(k, _):
                chunk_to_middle(c, (chip + k) % CHIPS)
                return 0
            lax.fori_loop(0, CHIPS, later, 0)

    def await_bytes(ref, sem):
        pltpu.make_async_copy(ref, ref, sem).wait()

    @pl.when(second_core)
    def _():
        for c in range(CHUNKS):
            rows = rows_of(c)
            await_bytes(mid[c], recv1.at[c])
            if c == 0:
                await_bytes(pb_mid, recv_pb)
            acouple, couple = mat_ref[3, rows], mat_ref[4, rows]

            def block(d):
                i = tbl[IDX2, lane_of(d)]
                s, h = i // 2, i % 2
                first = pb_mid[s, pl.ds(h, 1), :]
                second = pb_mid[s, pl.ds(2 + h, 1), :]
                return mid[c][i] + acouple * first + couple * second

            def body(k, _):
                d = (own + k) % slabs
                stage2[d, rows] = block(d)
                pltpu.make_async_remote_copy(
                    src_ref=stage2.at[d, rows], dst_ref=got[c].at[chip], send_sem=send2.at[c], recv_sem=recv2.at[c],
                    device_id={"slab": d}, device_id_type=MESH,
                ).start()
                return 0
            lax.fori_loop(1, slabs, body, 0)
            got[c][chip] = block(own)

    for c in range(CHUNKS):
        @pl.when(second_core)
        def _():
            await_bytes(got[c].at[pl.ds(0, CHIPS - 1)], recv2.at[c])

        @pl.when(first_core)
        def _():
            await_bytes(got[c], recv2.at[c])

        def gather(n, _):
            for j in range(4):
                new_out[4 * n + j, rows_of(c)] = got[c][tbl[IDX3 + 4 * n + j, 0]]
            return 0
        lax.fori_loop(0, NEW // 4, gather, 0)

    for i, (ok, dr, dc) in enumerate(neighbours):
        @pl.when(ok)
        def _():
            copy_of(i, dr, dc).wait_send()

    @pl.when(first_core)
    def _():
        for c in range(CHUNKS):
            await_bytes(stage1.at[:, rows_of(c)], send1.at[c])
        await_bytes(pb_stage, send_pb)

    @pl.when(second_core)
    def _():
        for c in range(CHUNKS):
            await_bytes(stage2.at[pl.ds(0, 2 * CHIPS - 1), rows_of(c)], send2.at[c])


def solution(mesh):
    slabs, cols = mesh.shape["slab"], mesh.shape["col"]

    def shards(pressure, storage, trans, source, shells_old, cap, tr, new_source, cell_block):
        vmem = pl.BlockSpec(memory_space=pltpu.VMEM)
        p, new = pl.pallas_call(
            functools.partial(move_kernel, slabs, cols),
            out_shape=(
                jax.ShapeDtypeStruct((64, 256), F32),
                jax.ShapeDtypeStruct((NEW, SH, 128), F32),
            ),
            in_specs=[pl.BlockSpec(memory_space=pl.ANY)] * 9,
            out_specs=[vmem] * 2,
            scratch_shapes=[
                pltpu.VMEM((16, 128), I32),
                pltpu.VMEM((1, SH), F32),
                pltpu.VMEM((1, SH), F32),
                pltpu.VMEM((1, OLD), I32),
                pltpu.VMEM((OLD, SH, 128), F32),
                pltpu.VMEM((6, SH, 128), F32),
                pltpu.VMEM((56, 128), I32),
                pltpu.SMEM((56, 128), I32),
                pltpu.VMEM((NF, 64, 256), F32),
                pltpu.VMEM((NF, HALO, 256), F32),
                pltpu.VMEM((64, 128), F32),
                pltpu.VMEM((64, 128), F32),
                pltpu.VMEM((80, 128), F32),
                pltpu.VMEM((80, 128), F32),
                pltpu.VMEM((64, 256), F32),
                pltpu.VMEM((64, 256), F32),
                pltpu.VMEM((OLD, 128), F32),
                pltpu.VMEM((OLD, 128), F32),
                pltpu.VMEM((2 * CHIPS, SH, 128), F32),
                tuple(pltpu.VMEM((2 * CHIPS, part, 128), F32) for part in PARTS),
                pltpu.VMEM((2 * CHIPS, SH, 128), F32),
                tuple(pltpu.VMEM((CHIPS, part, 128), F32) for part in PARTS),
                pltpu.VMEM((CHIPS, 8, 128), F32),
                pltpu.VMEM((CHIPS, 8, 128), F32),
                pltpu.SemaphoreType.DMA((8,)),
                pltpu.SemaphoreType.DMA,
                pltpu.SemaphoreType.DMA,
                pltpu.SemaphoreType.DMA((8,)),
                pltpu.SemaphoreType.DMA((8,)),
                pltpu.SemaphoreType.DMA((CHUNKS,)),
                pltpu.SemaphoreType.DMA((CHUNKS,)),
                pltpu.SemaphoreType.DMA,
                pltpu.SemaphoreType.DMA,
                pltpu.SemaphoreType.DMA((CHUNKS,)),
                pltpu.SemaphoreType.DMA((CHUNKS,)),
            ],
            compiler_params=pltpu.CompilerParams(
                collective_id=0, has_side_effects=True, vmem_limit_bytes=40 << 20
            ),
        )(
            *(pltpu.with_memory_space_constraint(x, pltpu.HBM) for x in (
                new_source.reshape(16, 128), cap.reshape(1, SH), tr.reshape(1, SH), cell_block,
                pressure, storage, trans, source, shells_old[0],
            ))
        )
        return p, new[None]

    f = P("slab", "col")
    return jax.shard_map(
        shards,
        mesh=mesh,
        in_specs=(f, f, f, f, P("col", "slab", None, None), P(), P(), P("col", None), P("col", "slab")),
        out_specs=(f, P("col", "slab", None, None)),
        check_vma=False,
    )
```
